32 devices in a mesh: aux: 4 (over y, x), pair: 8 (over z, core).
Axes of the slice: x: 2, y: 2, z: 4, core: 2. Of those that a mesh axis runs over, the one named last changes fastest.
Arguments:
- orbital_slabs: bfloat16 [32, 1024, 768], P('pair', 'aux'), may hold values from -2.5 to 2.5
- pno_maps: bfloat16 [128, 768, 256], P('pair'), may hold values from -0.21875 to 0.21875
- intersections: bfloat16 [128, 8, 256, 256], P('pair', 'aux'), may hold values from -0.375 to 0.375
- pno_energy: float32 [128, 256], P('pair'), may hold values from 0.25 to 2
- occ_energy: float32 [32], replicated, may hold values from -1 to -0.25
- pair_orbitals: int32 [128, 2], replicated, may hold values from 0 to 31, as said below
- partners: int32 [128, 8], replicated, may hold values from 0 to 127, as said below
- live: int32 [128], P('pair'), may hold values from 0 to 1, as said below
Outputs:
- amplitudes: bfloat16 [128, 256, 256], P('pair')
- pair_energy: float32 [128], P('pair')
The draws below stay inside these ranges and needn't reach their ends.
Inputs may be any that keep to these rules, and one draw needn't show every extreme that they name: `pair_orbitals`: each pair names two different orbitals. The pairs of one cluster of 16 slots (padding slots too) name at most one orbital of each block of 4 consecutive orbitals. `partners`: every partner is a live pair. All 128 partner entries of one cluster of 16 slots together name at most one pair of each cluster. In each cluster of 16 slots the live pairs come first and there is at least one; some cluster is full.
All inputs are finite; a program needn't handle non-finite values.
Results may differ from the reference program's by a relative error of at most 0.0066.
Values may be sent and summed in bfloat16 or wider, within the bound.
A program may use at most 128 MiB of HBM per device.

```python
import math
import jax
import jax.numpy as jnp
from jax import lax

VIRT = 768
AUX = 1024
PNO = 256
PARTNERS = 8
ITERS = 2
ORB_DEV = 4
PAIR_DEV = 16
ORBITALS = 32
PAIRS = 128


def draw_tables(key):
    clusters = PAIRS // PAIR_DEV
    owners = ORBITALS // ORB_DEV
    keys = jax.random.split(jax.random.fold_in(key, 4242), 7)
    lowest = max(1, PAIR_DEV // 4)
    counts = jax.random.randint(keys[0], (clusters,), lowest, PAIR_DEV + 1)
    fullest = jax.random.randint(keys[1], (), 0, clusters)
    counts = jnp.where(jnp.arange(clusters) == fullest, PAIR_DEV, counts).astype(jnp.int32)
    slot_index = jnp.arange(PAIRS) % PAIR_DEV
    cluster_of = jnp.arange(PAIRS) // PAIR_DEV
    live_slots = (slot_index < counts[cluster_of]).astype(jnp.int32)
    orbital_pool = jnp.arange(owners)[None, :] * ORB_DEV + jax.random.randint(keys[2], (clusters, owners), 0, ORB_DEV)
    first_owner = jax.random.randint(keys[3], (PAIRS,), 0, owners)
    second_owner = (first_owner + 1 + jax.random.randint(keys[4], (PAIRS,), 0, owners - 1)) % owners
    orbitals = jnp.stack([orbital_pool[cluster_of, first_owner], orbital_pool[cluster_of, second_owner]], axis=1).astype(jnp.int32)
    chosen_slot = jax.random.randint(keys[5], (clusters, clusters), 0, counts[None, :])
    partner_source = jax.random.randint(keys[6], (PAIRS, PARTNERS), 0, clusters)
    partner_ids = partner_source * PAIR_DEV + chosen_slot[cluster_of[:, None], partner_source]
    return (orbitals, partner_ids.astype(jnp.int32), live_slots)


def draw_pair_orbitals(key, part):
    return draw_tables(key)[0]


def draw_partners(key, part):
    return draw_tables(key)[1]


def draw_live(key, part):
    return draw_tables(key)[2]


def block_scale(stream_key, dims, pieces, low, top_value):
    gain = 1.0
    for axis_at, blocks in pieces:
        heights = jax.random.uniform(jax.random.fold_in(jax.random.fold_in(stream_key, 6), axis_at), (blocks,), jnp.float32, low / len(pieces), top_value / len(pieces))
        gain = gain * jnp.repeat(jnp.exp(heights), dims[axis_at] // blocks).reshape((-1,) + (1,) * (len(dims) - 1 - axis_at))
    return gain


def scatter_about(rng, extent, width, bound, cuts=(), kind=jnp.bfloat16):
    entries = width * jax.random.normal(rng, extent, jnp.float32)
    if cuts:
        entries = entries * block_scale(rng, extent, cuts, -0.22, 0.18)
    return jnp.clip(entries, -bound, bound).astype(kind)


def setup_inputs(seed: int = 0) -> dict:
    key_of = jax.random.split(jax.random.key(seed), 9)
    orbital_slabs = scatter_about(key_of[0], (ORBITALS, AUX, VIRT), 0.18, 2.5, ((0, 8), (1, 4)))
    pno_maps = scatter_about(key_of[1], (PAIRS, VIRT, PNO), VIRT ** -0.5, 0.21875, ((0, 8),))
    intersections = scatter_about(key_of[2], (PAIRS, PARTNERS, PNO, PNO), PNO ** -0.5, 0.375, ((0, 8), (1, 4)))
    pno_energy = jnp.clip(jnp.exp(math.log(2.0) - 2.0794415 * jax.random.uniform(key_of[3], (PAIRS, PNO), jnp.float32) ** block_scale(key_of[3], (PAIRS, PNO), ((0, 8),), -0.2, 0.2)), 0.25, 2.0)
    occ_energy = jnp.clip(jax.random.uniform(key_of[4], (ORBITALS,), jnp.float32, -1.0, -0.25), -1.0, -0.25)
    pair_orbitals = draw_pair_orbitals(jax.random.fold_in(key_of[8], 71), 0)
    partners = draw_partners(jax.random.fold_in(key_of[8], 71), 0)
    live = draw_live(jax.random.fold_in(key_of[8], 71), 0)
    return dict(orbital_slabs=orbital_slabs, pno_maps=pno_maps, intersections=intersections, pno_energy=pno_energy, occ_energy=occ_energy, pair_orbitals=pair_orbitals, partners=partners, live=live)


damping = 0.7


def reference(orbital_slabs, pno_maps, intersections, pno_energy, occ_energy, pair_orbitals, partners, live):
    weights = live.astype(jnp.float32)[:, None, None]
    indices = jnp.arange(PAIRS, dtype=jnp.int32)

    def integrals(index):
        first = pair_orbitals[index, 0]
        second = pair_orbitals[index, 1]
        mapping = pno_maps[index]
        left = jnp.dot(orbital_slabs[first], mapping, preferred_element_type=jnp.float32).astype(jnp.bfloat16)
        right = jnp.dot(orbital_slabs[second], mapping, preferred_element_type=jnp.float32).astype(jnp.bfloat16)
        return jnp.dot(left.T, right, preferred_element_type=jnp.float32)

    coulomb = lax.map(integrals, indices)
    coulomb_half = coulomb.astype(jnp.bfloat16)
    occupied = occ_energy[pair_orbitals[:, 0]] + occ_energy[pair_orbitals[:, 1]]
    denominator = pno_energy[:, :, None] + pno_energy[:, None, :] - occupied[:, None, None]
    amplitude = -weights * coulomb / denominator
    for sweep in range(ITERS):
        amp_half = amplitude.astype(jnp.bfloat16)

        def coupling(index):
            fetched = amp_half[partners[index]].astype(jnp.float32)
            intersection = intersections[index].astype(jnp.float32)
            rotated = jnp.einsum("rab,rbc->rac", intersection, fetched)
            rotated = lax.optimization_barrier(rotated.astype(jnp.bfloat16)).astype(jnp.float32)
            return jnp.einsum("rac,rdc->ad", rotated, intersection)

        coupled = lax.map(coupling, indices)
        amp_wide = amp_half.astype(jnp.float32)
        product = jnp.einsum("pab,pcb->pac", amp_wide, coulomb_half.astype(jnp.float32))
        product = lax.optimization_barrier(product.astype(jnp.bfloat16)).astype(jnp.float32)
        quadratic = jnp.einsum("pac,pcd->pad", product, amp_wide) / PNO
        residual = coulomb + denominator * amplitude - coupled + quadratic
        amplitude = weights * (amplitude - damping * residual / denominator)
    energy = weights[:, 0, 0] * jnp.sum(coulomb * amplitude, axis=(1, 2))
    return amplitude.astype(jnp.bfloat16), energy
```

```python
import functools

import jax
import jax.numpy as jnp
from jax import lax
from jax.experimental import pallas as pl
from jax.experimental.pallas import tpu as pltpu
from jax.sharding import PartitionSpec as P

ITERS = 2
CHUNKS = 4
damping = 0.7
BF16 = jnp.bfloat16
F32 = jnp.float32


def dot(x, y, dims):
    return lax.dot_general(x, y, ((dims[:1], dims[1:]), ((), ())), preferred_element_type=F32)


def kernel(
    groups, clusters, table, orbitals, refs, live, occ, slab, energy, maps_hbm, inter_hbm,
    out_hbm, energy_out, *scratch
):
    scratch = list(scratch)

    def take(count):
        got = scratch[:count]
        del scratch[:count]
        return got

    staged, incoming = take(CHUNKS), take(CHUNKS)
    (maps, inter, left, right, part_out, part_in, coulomb, coulomb_half, denom, rden) = take(10)
    (amp, half, energy_row) = take(3)
    split, quarter, zout, zin, fetched = (take(ITERS) for _ in range(5))
    (
        maps_sem, inter_send, inter_recv, slab_send, slab_recv, part_send, part_recv, split_send,
        split_recv, z_send, z_recv, f_send, f_recv, out_send, out_recv, e_send, e_recv,
    ) = scratch

    row = lax.axis_index("aux")
    cluster = lax.axis_index("pair")
    pair_count, virt, width = maps.shape
    share = pair_count // groups
    orb_count = slab.shape[0]
    local_cols = inter.shape[2]
    ref_cols = groups * local_cols
    chunk = slab.shape[1] // CHUNKS
    piece = width // groups

    def remote(src, dst, send, recv, **where):
        return pltpu.make_async_remote_copy(
            src_ref=src, dst_ref=dst, send_sem=send, recv_sem=recv, device_id=where,
            device_id_type=pl.DeviceIdType.MESH,
        )

    def loop(count, body):
        def step(i, carry):
            body(i)
            return carry

        lax.fori_loop(0, count, step, 0)

    def to_pair(i):
        return lax.rem(cluster + i, clusters)

    def from_pair(i):
        return lax.rem(cluster + clusters - i, clusters)

    def to_aux(i):
        return lax.rem(row + i, groups)

    def from_aux(i):
        return lax.rem(row + groups - i, groups)

    def far_first(j):
        return lax.rem(clusters // 2 - 1 + j, clusters - 1) + 1

    barrier = pltpu.get_barrier_semaphore()
    for i in range(1, clusters):
        pl.semaphore_signal(
            barrier, inc=1, device_id={"pair": to_pair(i)}, device_id_type=pl.DeviceIdType.MESH
        )
    for i in range(1, groups):
        pl.semaphore_signal(
            barrier, inc=1, device_id={"aux": to_aux(i)}, device_id_type=pl.DeviceIdType.MESH
        )
    maps_copy = pltpu.make_async_copy(maps_hbm, maps, maps_sem.at[0])
    maps_copy.start()
    inter_own = pltpu.make_async_copy(
        inter_hbm.at[pl.ds(row * share, share)], inter.at[row], maps_sem.at[1]
    )
    inter_own.start()
    pl.semaphore_wait(barrier, clusters + groups - 2)

    def slab_copy(k, i, source):
        return remote(
            staged[k].at[to_pair(i)], incoming[k].at[source], slab_send.at[k, i],
            slab_recv.at[k, i], pair=to_pair(i),
        )

    for k in range(CHUNKS):
        rows = slice(k * chunk, (k + 1) * chunk)

        def send_slab(j, k=k, rows=rows):
            i = far_first(j)
            to = to_pair(i)
            staged[k][to] = slab[table[to], rows, :]
            slab_copy(k, i, cluster).start()

        loop(clusters - 1, send_slab)
        incoming[k][cluster] = slab[table[cluster], rows, :]

    def inter_copy(i, source):
        return remote(
            inter_hbm.at[pl.ds(to_aux(i) * share, share)], inter.at[source], inter_send.at[i],
            inter_recv.at[i], aux=to_aux(i),
        )

    for i in range(1, groups):
        inter_copy(i, row).start()

    def denominators(q):
        p = cluster * pair_count + row * share + q
        occupied = occ[orbitals[2 * p]] + occ[orbitals[2 * p + 1]]
        across = jnp.broadcast_to(energy[row * share + q], (width, width))
        value = across + across.T - occupied
        denom[q] = value
        rden[q] = 1.0 / value

    loop(share, denominators)
    maps_copy.wait()

    def project(k, p):
        first = orbitals[2 * (cluster * pair_count + p)] // orb_count
        second = orbitals[2 * (cluster * pair_count + p) + 1] // orb_count
        both = jnp.concatenate([incoming[k][first], incoming[k][second]], axis=0)
        both = dot(both, maps[p], (1, 0)).astype(BF16)
        rows = slice(k * chunk, (k + 1) * chunk)
        left[p, rows, :] = both[:chunk]
        right[p, rows, :] = both[chunk:]

    def part_copy(i, q):
        return remote(
            part_out.at[i - 1, q], part_in.at[i - 1, q], part_send.at[i, q], part_recv.at[i, q],
            aux=to_aux(i),
        )

    for k in range(CHUNKS):
        loop(clusters - 1, lambda j, k=k: slab_copy(k, far_first(j), from_pair(far_first(j))).wait_recv())
        if k < CHUNKS - 1:
            loop(pair_count, lambda p, k=k: project(k, p))

    last = CHUNKS - 1
    for i in range(1, groups):

        def send_part(q, i=i):
            p = to_aux(i) * share + q
            project(last, p)
            part_out[i - 1, q] = dot(left[p], right[p], (0, 0)).astype(BF16)
            part_copy(i, q).start()

        loop(share, send_part)

    def own_part(q):
        p = row * share + q
        project(last, p)
        coulomb[q] = dot(left[p], right[p], (0, 0))

    loop(share, own_part)

    def split_copy(t, i, source):
        return remote(
            split[t].at[to_aux(i)], quarter[t].at[pl.ds(source * share, share)],
            split_send.at[t, i], split_recv.at[t, i], aux=to_aux(i),
        )

    def z_copy(t, i, source):
        return remote(
            zout[t].at[to_pair(i)], zin[t].at[source], z_send.at[t, i], z_recv.at[t, i],
            pair=to_pair(i),
        )

    def f_copy(t, i, j, member, source):
        return remote(
            zin[t].at[member], fetched[t].at[member, source], f_send.at[t, i, j],
            f_recv.at[t, i, j], aux=to_aux(i),
        )

    def weight(q):
        return live[row * share + q].astype(F32)

    def set_half(t, q, value):
        rounded = value.astype(BF16)
        half[q] = rounded
        for b in range(groups):
            split[t][b, q] = rounded[b * piece:(b + 1) * piece]

    def start_amplitude(q):
        for i in range(1, groups):
            part_copy(i, q).wait_recv()
        total = coulomb[q]
        for i in range(1, groups):
            total = total + part_in[i - 1, q].astype(F32)
        coulomb[q] = total
        coulomb_half[q] = total.astype(BF16)
        value = -weight(q) * total * rden[q]
        amp[q] = value
        set_half(0, q, value)

    loop(share, start_amplitude)

    for t in range(ITERS):
        for i in range(1, groups):
            split_copy(t, i, row).start()

        def keep(q, t=t):
            quarter[t][row * share + q] = split[t][row, q]

        loop(share, keep)

        def quadratic(q):
            product = dot(half[q], coulomb_half[q], (1, 1)).astype(BF16)
            settled = dot(product, half[q], (1, 0)) * (1.0 / width)
            before = amp[q]
            residual = coulomb[q] + denom[q] * before + settled
            amp[q] = before - damping * residual * rden[q]

        for i in range(1, groups):
            split_copy(t, i, from_aux(i)).wait_recv()

        def send_z(j, t=t):
            i = far_first(j)
            to = to_pair(i)
            zout[t][to] = quarter[t][table[clusters + to]]
            z_copy(t, i, cluster).start()

        loop(clusters - 1, send_z)
        mine = quarter[t][table[clusters + cluster]]
        zin[t][cluster] = mine
        fetched[t][cluster, row] = mine
        for i in range(1, groups):
            f_copy(t, i, 0, cluster, row).start()
        loop(share, quadratic)

        def forward(j, t=t):
            j = j + 1
            member = from_pair(j)
            z_copy(t, j, member).wait_recv()
            for i in range(1, groups):
                f_copy(t, i, j, member, row).start()
            fetched[t][member, row] = zin[t][member]

        loop(clusters - 1, forward)
        if t == 0:
            inter_own.wait()
            for i in range(1, groups):
                inter_copy(i, from_aux(i)).wait_recv()

        def arrive(j, t=t):
            for i in range(1, groups):
                f_copy(t, i, j, from_pair(j), from_aux(i)).wait_recv()

        loop(clusters, arrive)

        def update(q, t=t):
            p = cluster * pair_count + row * share + q
            coupled = jnp.zeros((width, width), F32)
            for r in range(ref_cols):
                source = refs[p * ref_cols + r] // pair_count
                overlap = inter[r // local_cols, q, r % local_cols]
                partner = fetched[t][source].reshape(width, width)
                rotated = dot(overlap, partner, (1, 0)).astype(BF16)
                coupled = coupled + dot(rotated, overlap, (1, 1))
            value = weight(q) * (amp[q] + damping * coupled * rden[q])
            if t < ITERS - 1:
                amp[q] = value
                set_half(t + 1, q, value)
            else:
                half[q] = value.astype(BF16)
                for i in range(1, groups):
                    out_copy(i, q, row).start()
                total = jnp.sum(coulomb[q] * value, axis=0, keepdims=True) * weight(q)
                energy_row[q] = total

        def out_copy(i, q, source):
            return remote(
                half.at[q], out_hbm.at[source * share + q], out_send.at[i, q], out_recv.at[i, q],
                aux=to_aux(i),
            )

        loop(share, update)

    out_own = pltpu.make_async_copy(half, out_hbm.at[pl.ds(row * share, share)], maps_sem.at[2])
    out_own.start()

    def e_copy(i, source):
        return remote(
            energy_row, energy_out.at[source], e_send.at[i], e_recv.at[i], aux=to_aux(i)
        )

    for i in range(1, groups):
        e_copy(i, row).start()
    energy_out[row] = energy_row[...]

    for k in range(CHUNKS):
        loop(clusters - 1, lambda j, k=k: slab_copy(k, j + 1, cluster).wait_send())
    for i in range(1, groups):
        inter_copy(i, row).wait_send()
        loop(share, lambda q, i=i: part_copy(i, q).wait_send())
    for t in range(ITERS):
        loop(clusters - 1, lambda j, t=t: z_copy(t, j + 1, cluster).wait_send())
        for i in range(1, groups):
            split_copy(t, i, row).wait_send()
            loop(clusters, lambda j, t=t, i=i: f_copy(t, i, j, from_pair(j), row).wait_send())
    for i in range(1, groups):
        loop(share, lambda q, i=i: out_copy(i, q, row).wait_send())
        loop(share, lambda q, i=i: out_copy(i, q, from_aux(i)).wait_recv())
        e_copy(i, row).wait_send()
        e_copy(i, from_aux(i)).wait_recv()
    out_own.wait()


def on_device(
    orbital_slabs, pno_maps, intersections, pno_energy, occ_energy, pair_orbitals, partners, live
):
    clusters = lax.axis_size("pair")
    groups = lax.axis_size("aux")
    cluster = lax.axis_index("pair")
    orb_count, aux_rows, virt = orbital_slabs.shape
    pair_count, _, width = pno_maps.shape
    cols = intersections.shape[1]
    share = pair_count // groups
    chunk = aux_rows // CHUNKS
    piece = width // groups
    wanted = pair_orbitals.reshape(clusters, -1)
    named = partners.reshape(clusters, -1)
    table = jnp.concatenate([
        jnp.max(jnp.where(wanted // orb_count == cluster, wanted % orb_count, 0), axis=1),
        jnp.max(jnp.where(named // pair_count == cluster, named % pair_count, 0), axis=1),
    ])
    square = (width, width)
    vm = pltpu.VMEM
    dma = lambda *shape: pltpu.SemaphoreType.DMA(shape)
    scratch = (
        [vm((clusters, chunk, virt), BF16)] * (2 * CHUNKS)
        + [
            vm((pair_count, virt, width), BF16),
            vm((groups, share, cols) + square, BF16),
            vm((pair_count, aux_rows, width), BF16),
            vm((pair_count, aux_rows, width), BF16),
            vm((groups - 1, share) + square, BF16),
            vm((groups - 1, share) + square, BF16),
            vm((share,) + square, F32),
            vm((share,) + square, BF16),
            vm((share,) + square, F32),
            vm((share,) + square, F32),
            vm((share,) + square, F32),
            vm((share,) + square, BF16),
            vm((share, 1, width), F32),
        ]
        + [vm((groups, share, piece, width), BF16)] * ITERS
        + [vm((pair_count, piece, width), BF16)] * ITERS
        + [vm((clusters, piece, width), BF16)] * (2 * ITERS)
        + [vm((clusters, groups, piece, width), BF16)] * ITERS
        + [
            dma(3), dma(groups), dma(groups), dma(CHUNKS, clusters), dma(CHUNKS, clusters),
            dma(groups, share), dma(groups, share), dma(ITERS, groups), dma(ITERS, groups),
            dma(ITERS, clusters), dma(ITERS, clusters), dma(ITERS, groups, clusters),
            dma(ITERS, groups, clusters), dma(groups, share), dma(groups, share), dma(groups),
            dma(groups),
        ]
    )
    smem = pl.BlockSpec(memory_space=pltpu.SMEM)
    vmem = pl.BlockSpec(memory_space=pltpu.VMEM)
    anywhere = pl.BlockSpec(memory_space=pl.ANY)
    result, energy = pl.pallas_call(
        functools.partial(kernel, groups, clusters),
        out_shape=(
            jax.ShapeDtypeStruct((pair_count,) + square, BF16),
            jax.ShapeDtypeStruct((groups, share, 1, width), F32),
        ),
        in_specs=[smem] * 5 + [vmem, vmem, anywhere, anywhere],
        out_specs=(anywhere, vmem),
        scratch_shapes=scratch,
        compiler_params=pltpu.CompilerParams(
            collective_id=0, has_side_effects=True, vmem_limit_bytes=62 << 20
        ),
        name="local_pair_amplitudes",
    )(
        table, pair_orbitals.reshape(-1), partners.reshape(-1), live, occ_energy, orbital_slabs,
        pno_energy.reshape(pair_count, 1, width), pno_maps, intersections,
    )
    return result, jnp.sum(energy, axis=(2, 3)).reshape(-1)


def solution(mesh):
    placed = (
        P("pair", "aux", None),
        P("pair", None, None),
        P("pair", "aux", None, None),
        P("pair", None),
        P(),
        P(),
        P(),
        P("pair"),
    )
    return jax.shard_map(
        on_device,
        mesh=mesh,
        in_specs=placed,
        out_specs=(P("pair", None, None), P("pair")),
        check_vma=False,
    )
```

```python
import functools

import jax
import jax.numpy as jnp
from jax import lax
from jax.experimental import pallas as pl
from jax.experimental.pallas import tpu as pltpu
from jax.sharding import PartitionSpec as P

ITERS = 2
PARTS = (5, 5, 3, 3)
CHUNKS = len(PARTS)
HEAD = 2
damping = 0.7
BF16 = jnp.bfloat16
F32 = jnp.float32


def dot(x, y, dims):
    return lax.dot_general(x, y, ((dims[:1], dims[1:]), ((), ())), preferred_element_type=F32)


def kernel(
    groups, clusters, orbitals, refs, live, occ, slab, energy, maps_hbm, inter_hbm,
    out_hbm, energy_out, *scratch
):
    scratch = list(scratch)

    def take(count):
        got = scratch[:count]
        del scratch[:count]
        return got

    staged, incoming = take(CHUNKS), take(CHUNKS)
    tail_out, tail_in = take(CHUNKS - HEAD), take(CHUNKS - HEAD)
    (table, maps, inter, left, right, part_out, part_in, coulomb, coulomb_half, denom, rden) = take(11)
    (amp, half, energy_row) = take(3)
    split, quarter, zout, zin = (take(ITERS) for _ in range(4))
    (fetched,) = take(1)
    (
        maps_sem, inter_send, inter_recv, slab_send, slab_recv, part_send, part_recv, tail_send, tail_recv, split_send,
        split_recv, z_send, z_recv, f_send, f_recv, out_send, out_recv, e_send, e_recv,
    ) = scratch

    row = lax.axis_index("aux")
    cluster = lax.axis_index("pair")
    pair_count, virt, width = maps.shape
    share = pair_count // groups
    orb_count = slab.shape[0]
    local_cols = inter.shape[2]
    ref_cols = groups * local_cols
    unit = slab.shape[1] // sum(PARTS)
    starts = [sum(PARTS[:k]) * unit for k in range(CHUNKS + 1)]
    piece = width // groups

    def remote(src, dst, send, recv, **where):
        return pltpu.make_async_remote_copy(
            src_ref=src, dst_ref=dst, send_sem=send, recv_sem=recv, device_id=where,
            device_id_type=pl.DeviceIdType.MESH,
        )

    def loop(count, body):
        def step(i, carry):
            body(i)
            return carry

        lax.fori_loop(0, count, step, 0)

    def to_pair(i):
        return lax.rem(cluster + i, clusters)

    def from_pair(i):
        return lax.rem(cluster + clusters - i, clusters)

    def to_aux(i):
        return lax.rem(row + i, groups)

    def from_aux(i):
        return lax.rem(row + groups - i, groups)

    def far_first(j):
        return lax.rem(clusters // 2 - 1 + j, clusters - 1) + 1

    barrier = pltpu.get_barrier_semaphore()
    for i in range(1, clusters):
        pl.semaphore_signal(
            barrier, inc=1, device_id={"pair": to_pair(i)}, device_id_type=pl.DeviceIdType.MESH
        )
    for i in range(1, groups):
        pl.semaphore_signal(
            barrier, inc=1, device_id={"aux": to_aux(i)}, device_id_type=pl.DeviceIdType.MESH
        )
    maps_copy = pltpu.make_async_copy(maps_hbm, maps, maps_sem.at[0])
    maps_copy.start()
    inter_own = pltpu.make_async_copy(
        inter_hbm.at[pl.ds(row * share, share)], inter.at[row], maps_sem.at[1]
    )
    inter_own.start()

    def scan_orbitals(c):
        found = 0
        for n in range(pair_count):
            for side in range(2):
                at = orbitals[side, c * pair_count + n] - cluster * orb_count
                found = jnp.where((at >= 0) & (at < orb_count), at, found)
        table[c] = found

    def scan_pairs(c):
        found = 0
        for n in range(pair_count):
            for r in range(ref_cols):
                at = refs[r, c * pair_count + n] - cluster * pair_count
                found = jnp.where((at >= 0) & (at < pair_count), at, found)
        table[clusters + c] = found

    loop(clusters, scan_orbitals)
    pl.semaphore_wait(barrier, clusters + groups - 2)

    def slab_copy(k, i, source):
        return remote(
            staged[k].at[to_pair(i)], incoming[k].at[source], slab_send.at[k, i],
            slab_recv.at[k, i], pair=to_pair(i),
        )

    for k in range(CHUNKS):
        rows = slice(starts[k], starts[k + 1])

        def send_slab(j, k=k, rows=rows):
            i = far_first(j)
            to = to_pair(i)
            staged[k][to] = slab[table[to], rows, :]
            slab_copy(k, i, cluster).start()

        loop(clusters - 1, send_slab)
        incoming[k][cluster] = slab[table[cluster], rows, :]

    def inter_copy(i, source):
        return remote(
            inter_hbm.at[pl.ds(to_aux(i) * share, share)], inter.at[source], inter_send.at[i],
            inter_recv.at[i], aux=to_aux(i),
        )

    for i in range(1, groups):
        inter_copy(i, row).start()

    def denominators(q):
        p = cluster * pair_count + row * share + q
        occupied = occ[orbitals[0, p]] + occ[orbitals[1, p]]
        across = jnp.broadcast_to(energy[pl.ds(row * share + q, 1), :], (width, width))
        value = across + across.T - occupied
        denom[q] = value
        rden[q] = 1.0 / value

    loop(share, denominators)
    loop(clusters, scan_pairs)
    maps_copy.wait()

    def project(k, p):
        first = orbitals[0, cluster * pair_count + p] // orb_count
        second = orbitals[1, cluster * pair_count + p] // orb_count
        both = jnp.concatenate([incoming[k][first], incoming[k][second]], axis=0)
        return dot(both, maps[p], (1, 0)).astype(BF16)

    def project_head(k, p):
        both = project(k, p)
        count = starts[k + 1] - starts[k]
        left[p, starts[k]:starts[k + 1], :] = both[:count]
        right[p, starts[k]:starts[k + 1], :] = both[count:]

    def part_copy(i, q):
        return remote(
            part_out.at[i - 1, q], part_in.at[i - 1, q], part_send.at[i, q], part_recv.at[i, q],
            aux=to_aux(i),
        )

    def tail_copy(k, i, q):
        return remote(
            tail_out[k - HEAD].at[i - 1, q], tail_in[k - HEAD].at[i, q],
            tail_send.at[k - HEAD, i, q], tail_recv.at[k - HEAD, i, q], aux=to_aux(i),
        )

    def send_part(q):
        for i in range(1, groups):
            p = to_aux(i) * share + q
            project_head(HEAD - 1, p)
            part_out[i - 1, q] = dot(left[p], right[p], (0, 0)).astype(BF16)
            part_copy(i, q).start()
        p = row * share + q
        project_head(HEAD - 1, p)
        coulomb[q] = dot(left[p], right[p], (0, 0))

    def send_tail(k, q):
        for i in range(1, groups):
            tail_out[k - HEAD][i - 1, q] = project(k, to_aux(i) * share + q)
            tail_copy(k, i, q).start()
        tail_in[k - HEAD][0, q] = project(k, row * share + q)

    for k in range(CHUNKS):
        loop(clusters - 1, lambda j, k=k: slab_copy(k, far_first(j), from_pair(far_first(j))).wait_recv())
        if k < HEAD - 1:
            loop(pair_count, lambda p, k=k: project_head(k, p))
        elif k == HEAD - 1:
            loop(share, send_part)
        else:
            loop(share, lambda q, k=k: send_tail(k, q))

    def split_copy(t, i, q, source):
        return remote(
            split[t].at[to_aux(i), q], quarter[t].at[source * share + q],
            split_send.at[t, i, q], split_recv.at[t, i, q], aux=to_aux(i),
        )

    def z_copy(t, i, source):
        return remote(
            zout[t].at[to_pair(i)], zin[t].at[source], z_send.at[t, i], z_recv.at[t, i],
            pair=to_pair(i),
        )

    def f_copy(t, i, j, member, source):
        return remote(
            zin[t].at[member], fetched.at[member, source], f_send.at[t, i, j],
            f_recv.at[t, i, j], aux=to_aux(i),
        )

    def weight(q):
        return live[row * share + q].astype(F32)

    def set_half(t, q, value):
        rounded = value.astype(BF16)
        half[q] = rounded
        for b in range(groups):
            split[t][b, q] = rounded[b * piece:(b + 1) * piece]
        for i in range(1, groups):
            split_copy(t, i, q, row).start()
        quarter[t][row * share + q] = split[t][row, q]

    def start_amplitude(q):
        for i in range(1, groups):
            part_copy(i, q).wait_recv()
        total = coulomb[q]
        for i in range(1, groups):
            total = total + part_in[i - 1, q].astype(F32)
        lefts, rights = [], []
        for k in range(HEAD, CHUNKS):
            count = starts[k + 1] - starts[k]
            for i in range(groups):
                if i:
                    tail_copy(k, i, q).wait_recv()
                lefts.append(tail_in[k - HEAD][i, q, :count, :])
                rights.append(tail_in[k - HEAD][i, q, count:, :])
        total = total + dot(jnp.concatenate(lefts, 0), jnp.concatenate(rights, 0), (0, 0))
        coulomb[q] = total
        coulomb_half[q] = total.astype(BF16)
        value = -weight(q) * total * rden[q]
        amp[q] = value
        set_half(0, q, value)

    loop(share, start_amplitude)

    for t in range(ITERS):
        def quadratic(q):
            product = dot(half[q], coulomb_half[q], (1, 1)).astype(BF16)
            settled = dot(product, half[q], (1, 0)) * (1.0 / width)
            before = amp[q]
            residual = coulomb[q] + denom[q] * before + settled
            amp[q] = before - damping * residual * rden[q]

        for i in range(1, groups):
            loop(share, lambda q, t=t, i=i: split_copy(t, i, q, from_aux(i)).wait_recv())

        def send_z(j, t=t):
            i = far_first(j)
            to = to_pair(i)
            zout[t][to] = quarter[t][table[clusters + to]]
            z_copy(t, i, cluster).start()

        loop(clusters - 1, send_z)
        mine = quarter[t][table[clusters + cluster]]
        zin[t][cluster] = mine
        fetched[cluster, row] = mine
        for i in range(1, groups):
            f_copy(t, i, 0, cluster, row).start()
        loop(share, quadratic)

        def forward(j, t=t):
            j = j + 1
            member = from_pair(j)
            z_copy(t, j, member).wait_recv()
            for i in range(1, groups):
                f_copy(t, i, j, member, row).start()
            fetched[member, row] = zin[t][member]

        loop(clusters - 1, forward)
        if t == 0:
            inter_own.wait()
            for i in range(1, groups):
                inter_copy(i, from_aux(i)).wait_recv()

        def arrive(j, t=t):
            for i in range(1, groups):
                f_copy(t, i, j, from_pair(j), from_aux(i)).wait_recv()

        loop(clusters, arrive)

        def update(q, t=t):
            p = cluster * pair_count + row * share + q
            coupled = jnp.zeros((width, width), F32)
            for r in range(ref_cols):
                source = refs[r, p] // pair_count
                overlap = inter[r // local_cols, q, r % local_cols]
                partner = fetched[source].reshape(width, width)
                rotated = dot(overlap, partner, (1, 0)).astype(BF16)
                coupled = coupled + dot(rotated, overlap, (1, 1))
            value = amp[q] + damping * coupled * rden[q]
            if t < ITERS - 1:
                value = weight(q) * value
                amp[q] = value
                set_half(t + 1, q, value)
            else:
                half[q] = value.astype(BF16)
                for i in range(1, groups):
                    out_copy(i, q, row).start()
                total = jnp.sum(coulomb[q] * value, axis=0, keepdims=True) * weight(q)
                energy_row[q] = total

        def out_copy(i, q, source):
            return remote(
                half.at[q], out_hbm.at[source * share + q], out_send.at[i, q], out_recv.at[i, q],
                aux=to_aux(i),
            )

        loop(share, update)

    out_own = pltpu.make_async_copy(half, out_hbm.at[pl.ds(row * share, share)], maps_sem.at[2])
    out_own.start()

    def e_copy(i, source):
        return remote(
            energy_row, energy_out.at[pl.ds(source * share, share)], e_send.at[i], e_recv.at[i], aux=to_aux(i)
        )

    for i in range(1, groups):
        e_copy(i, row).start()
    energy_out[pl.ds(row * share, share)] = energy_row[...]

    for k in range(CHUNKS):
        loop(clusters - 1, lambda j, k=k: slab_copy(k, j + 1, cluster).wait_send())
    for i in range(1, groups):
        inter_copy(i, row).wait_send()
        loop(share, lambda q, i=i: part_copy(i, q).wait_send())
        for k in range(HEAD, CHUNKS):
            loop(share, lambda q, i=i, k=k: tail_copy(k, i, q).wait_send())
    for t in range(ITERS):
        loop(clusters - 1, lambda j, t=t: z_copy(t, j + 1, cluster).wait_send())
        for i in range(1, groups):
            loop(share, lambda q, t=t, i=i: split_copy(t, i, q, row).wait_send())
            loop(clusters, lambda j, t=t, i=i: f_copy(t, i, j, from_pair(j), row).wait_send())
    for i in range(1, groups):
        loop(share, lambda q, i=i: out_copy(i, q, row).wait_send())
        loop(share, lambda q, i=i: out_copy(i, q, from_aux(i)).wait_recv())
        e_copy(i, row).wait_send()
        e_copy(i, from_aux(i)).wait_recv()
    out_own.wait()


def on_device(
    orbital_slabs, pno_maps, intersections, pno_energy, occ_energy, pair_orbitals, partners, live
):
    clusters = lax.axis_size("pair")
    groups = lax.axis_size("aux")
    _, aux_rows, virt = orbital_slabs.shape
    pair_count, _, width = pno_maps.shape
    cols = intersections.shape[1]
    share = pair_count // groups
    unit = aux_rows // sum(PARTS)
    head_rows = sum(PARTS[:HEAD]) * unit
    tails = [2 * part * unit for part in PARTS[HEAD:]]
    piece = width // groups
    square = (width, width)
    vm = pltpu.VMEM
    dma = lambda *shape: pltpu.SemaphoreType.DMA(shape)
    scratch = (
        [vm((clusters, part * unit, virt), BF16) for part in PARTS] * 2
        + [vm((groups - 1, share, rows, width), BF16) for rows in tails]
        + [vm((groups, share, rows, width), BF16) for rows in tails]
        + [
            pltpu.SMEM((2 * clusters,), jnp.int32),
            vm((pair_count, virt, width), BF16),
            vm((groups, share, cols) + square, BF16),
            vm((pair_count, head_rows, width), BF16),
            vm((pair_count, head_rows, width), BF16),
            vm((groups - 1, share) + square, BF16),
            vm((groups - 1, share) + square, BF16),
            vm((share,) + square, F32),
            vm((share,) + square, BF16),
            vm((share,) + square, F32),
            vm((share,) + square, F32),
            vm((share,) + square, F32),
            vm((share,) + square, BF16),
            vm((share, 1, width), F32),
        ]
        + [vm((groups, share, piece, width), BF16)] * ITERS
        + [vm((pair_count, piece, width), BF16)] * ITERS
        + [vm((clusters, piece, width), BF16)] * (2 * ITERS)
        + [vm((clusters, groups, piece, width), BF16)]
        + [
            dma(3), dma(groups), dma(groups), dma(CHUNKS, clusters), dma(CHUNKS, clusters),
            dma(groups, share), dma(groups, share), dma(CHUNKS - HEAD, groups, share),
            dma(CHUNKS - HEAD, groups, share), dma(ITERS, groups, share), dma(ITERS, groups, share),
            dma(ITERS, clusters), dma(ITERS, clusters), dma(ITERS, groups, clusters),
            dma(ITERS, groups, clusters), dma(groups, share), dma(groups, share), dma(groups),
            dma(groups),
        ]
    )
    smem = pl.BlockSpec(memory_space=pltpu.SMEM)
    vmem = pl.BlockSpec(memory_space=pltpu.VMEM)
    anywhere = pl.BlockSpec(memory_space=pl.ANY)
    result, energy = pl.pallas_call(
        functools.partial(kernel, groups, clusters),
        out_shape=(
            jax.ShapeDtypeStruct((pair_count,) + square, BF16),
            jax.ShapeDtypeStruct((pair_count, 1, width), F32),
        ),
        in_specs=[smem] * 4 + [vmem, vmem, anywhere, anywhere],
        out_specs=(anywhere, vmem),
        scratch_shapes=scratch,
        compiler_params=pltpu.CompilerParams(
            collective_id=0, has_side_effects=True, vmem_limit_bytes=62 << 20
        ),
        name="local_pair_amplitudes",
    )(
        pair_orbitals.T, partners.T, live, occ_energy, orbital_slabs, pno_energy, pno_maps,
        intersections,
    )
    result = jnp.where(live[:, None, None] > 0, result, jnp.zeros_like(result))
    return result, jnp.sum(energy, axis=(1, 2))


def solution(mesh):
    placed = (
        P("pair", "aux", None),
        P("pair", None, None),
        P("pair", "aux", None, None),
        P("pair", None),
        P(),
        P(),
        P(),
        P("pair"),
    )
    return jax.shard_map(
        on_device,
        mesh=mesh,
        in_specs=placed,
        out_specs=(P("pair", None, None), P("pair")),
        check_vma=False,
    )
```

```python
import functools

import jax
import jax.numpy as jnp
from jax import lax
from jax.experimental import pallas as pl
from jax.experimental.pallas import tpu as pltpu
from jax.sharding import PartitionSpec as P

ITERS = 2
PARTS = (5, 5, 3, 3)
CHUNKS = len(PARTS)
HEAD = 2
damping = 0.7
BF16 = jnp.bfloat16
F32 = jnp.float32


def dot(x, y, dims):
    return lax.dot_general(x, y, ((dims[:1], dims[1:]), ((), ())), preferred_element_type=F32)


def kernel(
    groups, clusters, orbitals, refs, live, occ, slab, energy, maps_hbm, inter_hbm,
    out_hbm, energy_out, *scratch
):
    scratch = list(scratch)

    def take(count):
        got = scratch[:count]
        del scratch[:count]
        return got

    staged, incoming = take(CHUNKS), take(CHUNKS)
    tail_out, tail_in = take(CHUNKS - HEAD), take(CHUNKS - HEAD)
    (table, maps, inter, left, right, part_out, part_in, coulomb, coulomb_half, denom, rden) = take(11)
    (amp, half, energy_row) = take(3)
    split, quarter, zout, zin = (take(ITERS) for _ in range(4))
    (fetched,) = take(1)
    (
        maps_sem, inter_send, inter_recv, slab_send, slab_recv, part_send, part_recv, tail_send, tail_recv, split_send,
        split_recv, z_send, z_recv, f_send, f_recv, out_send, out_recv, e_send, e_recv,
    ) = scratch

    row = lax.axis_index("aux")
    cluster = lax.axis_index("pair")
    pair_count, virt, width = maps.shape
    share = pair_count // groups
    orb_count = slab.shape[0]
    local_cols = inter.shape[2]
    ref_cols = groups * local_cols
    unit = slab.shape[1] // sum(PARTS)
    starts = [sum(PARTS[:k]) * unit for k in range(CHUNKS + 1)]
    piece = width // groups

    def remote(src, dst, send, recv, **where):
        return pltpu.make_async_remote_copy(
            src_ref=src, dst_ref=dst, send_sem=send, recv_sem=recv, device_id=where,
            device_id_type=pl.DeviceIdType.MESH,
        )

    def loop(count, body):
        def step(i, carry):
            body(i)
            return carry

        lax.fori_loop(0, count, step, 0)

    def to_pair(i):
        return lax.rem(cluster + i, clusters)

    def from_pair(i):
        return lax.rem(cluster + clusters - i, clusters)

    def to_aux(i):
        return lax.rem(row + i, groups)

    def from_aux(i):
        return lax.rem(row + groups - i, groups)

    def far_first(j):
        return lax.rem(clusters // 2 - 1 + j, clusters - 1) + 1

    barrier = pltpu.get_barrier_semaphore()
    for i in range(1, clusters):
        pl.semaphore_signal(
            barrier, inc=1, device_id={"pair": to_pair(i)}, device_id_type=pl.DeviceIdType.MESH
        )
    for i in range(1, groups):
        pl.semaphore_signal(
            barrier, inc=1, device_id={"aux": to_aux(i)}, device_id_type=pl.DeviceIdType.MESH
        )
    maps_copy = pltpu.make_async_copy(maps_hbm, maps, maps_sem.at[0])
    maps_copy.start()
    inter_own = pltpu.make_async_copy(
        inter_hbm.at[pl.ds(row * share, share)], inter.at[row], maps_sem.at[1]
    )
    inter_own.start()

    def scan_orbitals(c):
        found = 0
        for n in range(pair_count):
            for side in range(2):
                at = orbitals[side, c * pair_count + n] - cluster * orb_count
                found = jnp.where((at >= 0) & (at < orb_count), at, found)
        table[c] = found

    def scan_pairs(c):
        found = 0
        for n in range(pair_count):
            for r in range(ref_cols):
                at = refs[r, c * pair_count + n] - cluster * pair_count
                found = jnp.where((at >= 0) & (at < pair_count), at, found)
        table[clusters + c] = found

    loop(clusters, scan_orbitals)
    pl.semaphore_wait(barrier, clusters + groups - 2)

    def slab_copy(k, i, source):
        return remote(
            staged[k].at[to_pair(i)], incoming[k].at[source], slab_send.at[k, i],
            slab_recv.at[k, i], pair=to_pair(i),
        )

    def inter_copy(i, q, source):
        return remote(
            inter_hbm.at[to_aux(i) * share + q], inter.at[source, q], inter_send.at[i, q],
            inter_recv.at[i, q], aux=to_aux(i),
        )

    window = (clusters - 1) // 2

    def issue(k):
        rows = slice(starts[k], starts[k + 1])
        pairs = range(k * share // HEAD, (k + 1) * share // HEAD) if k < HEAD else ()

        def send_slab(j):
            i = far_first(j)
            to = to_pair(i)
            staged[k][to] = slab[table[to], rows, :]
            slab_copy(k, i, cluster).start()

        loop(window, send_slab)
        for n, q in enumerate(pairs):
            for i in range(1, groups):
                inter_copy(i, q, row).start()
            if n == 0:
                loop(clusters - 1 - window, lambda j: send_slab(j + window))
        if not pairs:
            loop(clusters - 1 - window, lambda j: send_slab(j + window))
        incoming[k][cluster] = slab[table[cluster], rows, :]

    def issue_after(k):
        loop(window, lambda j: slab_copy(k, far_first(j), cluster).wait_send())
        issue(k + 1)

    issue(0)

    def denominators(q):
        p = cluster * pair_count + row * share + q
        occupied = occ[orbitals[0, p]] + occ[orbitals[1, p]]
        across = jnp.broadcast_to(energy[pl.ds(row * share + q, 1), :], (width, width))
        value = across + across.T - occupied
        denom[q] = value
        rden[q] = 1.0 / value

    loop(share, denominators)
    loop(clusters, scan_pairs)
    maps_copy.wait()
    issue_after(0)

    def project(k, p):
        first = orbitals[0, cluster * pair_count + p] // orb_count
        second = orbitals[1, cluster * pair_count + p] // orb_count
        both = jnp.concatenate([incoming[k][first], incoming[k][second]], axis=0)
        return dot(both, maps[p], (1, 0)).astype(BF16)

    def project_head(k, p):
        both = project(k, p)
        count = starts[k + 1] - starts[k]
        left[p, starts[k]:starts[k + 1], :] = both[:count]
        right[p, starts[k]:starts[k + 1], :] = both[count:]

    def part_copy(i, q):
        return remote(
            part_out.at[i - 1, q], part_in.at[i - 1, q], part_send.at[i, q], part_recv.at[i, q],
            aux=to_aux(i),
        )

    def tail_copy(k, i, q):
        return remote(
            tail_out[k - HEAD].at[i - 1, q], tail_in[k - HEAD].at[i, q],
            tail_send.at[k - HEAD, i, q], tail_recv.at[k - HEAD, i, q], aux=to_aux(i),
        )

    def send_part(q):
        for i in range(1, groups):
            p = to_aux(i) * share + q
            project_head(HEAD - 1, p)
            part_out[i - 1, q] = dot(left[p], right[p], (0, 0)).astype(BF16)
            part_copy(i, q).start()
        p = row * share + q
        project_head(HEAD - 1, p)
        coulomb[q] = dot(left[p], right[p], (0, 0))

    def send_tail(k, q):
        for i in range(1, groups):
            tail_out[k - HEAD][i - 1, q] = project(k, to_aux(i) * share + q)
            tail_copy(k, i, q).start()
        tail_in[k - HEAD][0, q] = project(k, row * share + q)

    for k in range(CHUNKS):
        loop(clusters - 1, lambda j, k=k: slab_copy(k, far_first(j), from_pair(far_first(j))).wait_recv())
        if 0 < k + 1 < CHUNKS - 1:
            issue_after(k + 1)
        if k < HEAD - 1:
            loop(pair_count, lambda p, k=k: project_head(k, p))
        elif k == HEAD - 1:
            loop(share, send_part)
        else:
            loop(share, lambda q, k=k: send_tail(k, q))

    def split_copy(t, i, q, source):
        return remote(
            split[t].at[to_aux(i), q], quarter[t].at[source * share + q],
            split_send.at[t, i, q], split_recv.at[t, i, q], aux=to_aux(i),
        )

    def z_copy(t, i, source):
        return remote(
            zout[t].at[to_pair(i)], zin[t].at[source], z_send.at[t, i], z_recv.at[t, i],
            pair=to_pair(i),
        )

    def f_copy(t, i, j, member, source):
        return remote(
            zin[t].at[member], fetched.at[member, source], f_send.at[t, i, j],
            f_recv.at[t, i, j], aux=to_aux(i),
        )

    def weight(q):
        return live[row * share + q].astype(F32)

    def set_half(t, q, value):
        rounded = value.astype(BF16)
        half[q] = rounded
        for b in range(groups):
            split[t][b, q] = rounded[b * piece:(b + 1) * piece]
        for i in range(1, groups):
            split_copy(t, i, q, row).start()
        quarter[t][row * share + q] = split[t][row, q]

    def start_amplitude(q):
        for i in range(1, groups):
            part_copy(i, q).wait_recv()
        total = coulomb[q]
        for i in range(1, groups):
            total = total + part_in[i - 1, q].astype(F32)
        lefts, rights = [], []
        for k in range(HEAD, CHUNKS):
            count = starts[k + 1] - starts[k]
            for i in range(groups):
                if i:
                    tail_copy(k, i, q).wait_recv()
                lefts.append(tail_in[k - HEAD][i, q, :count, :])
                rights.append(tail_in[k - HEAD][i, q, count:, :])
        total = total + dot(jnp.concatenate(lefts, 0), jnp.concatenate(rights, 0), (0, 0))
        coulomb[q] = total
        coulomb_half[q] = total.astype(BF16)
        value = -weight(q) * total * rden[q]
        amp[q] = value
        set_half(0, q, value)

    loop(share, start_amplitude)

    for t in range(ITERS):
        def quadratic(q):
            product = dot(half[q], coulomb_half[q], (1, 1)).astype(BF16)
            settled = dot(product, half[q], (1, 0)) * (1.0 / width)
            before = amp[q]
            residual = coulomb[q] + denom[q] * before + settled
            amp[q] = before - damping * residual * rden[q]

        for i in range(1, groups):
            loop(share, lambda q, t=t, i=i: split_copy(t, i, q, from_aux(i)).wait_recv())

        def send_z(j, t=t):
            i = far_first(j)
            to = to_pair(i)
            zout[t][to] = quarter[t][table[clusters + to]]
            z_copy(t, i, cluster).start()

        loop(clusters - 1, send_z)
        mine = quarter[t][table[clusters + cluster]]
        zin[t][cluster] = mine
        fetched[cluster, row] = mine
        for i in range(1, groups):
            f_copy(t, i, 0, cluster, row).start()
        loop(share, quadratic)

        def forward(j, t=t):
            j = j + 1
            member = from_pair(j)
            z_copy(t, j, member).wait_recv()
            for i in range(1, groups):
                f_copy(t, i, j, member, row).start()
            fetched[member, row] = zin[t][member]

        loop(clusters - 1, forward)
        if t == 0:
            inter_own.wait()
            for i in range(1, groups):
                loop(share, lambda q, i=i: inter_copy(i, q, from_aux(i)).wait_recv())

        def arrive(j, t=t):
            for i in range(1, groups):
                f_copy(t, i, j, from_pair(j), from_aux(i)).wait_recv()

        loop(clusters, arrive)

        def update(q, t=t):
            p = cluster * pair_count + row * share + q
            coupled = jnp.zeros((width, width), F32)
            for r in range(ref_cols):
                source = refs[r, p] // pair_count
                overlap = inter[r // local_cols, q, r % local_cols]
                partner = fetched[source].reshape(width, width)
                rotated = dot(overlap, partner, (1, 0)).astype(BF16)
                coupled = coupled + dot(rotated, overlap, (1, 1))
            value = amp[q] + damping * coupled * rden[q]
            value = weight(q) * value
            if t < ITERS - 1:
                amp[q] = value
                set_half(t + 1, q, value)
            else:
                half[q] = value.astype(BF16)
                for i in range(1, groups):
                    out_copy(i, q, row).start()
                total = jnp.sum(coulomb[q] * value, axis=0, keepdims=True)
                energy_row[q] = total

        def out_copy(i, q, source):
            return remote(
                half.at[q], out_hbm.at[source * share + q], out_send.at[i, q], out_recv.at[i, q],
                aux=to_aux(i),
            )

        loop(share, update)

    out_own = pltpu.make_async_copy(half, out_hbm.at[pl.ds(row * share, share)], maps_sem.at[2])
    out_own.start()

    def e_copy(i, source):
        return remote(
            energy_row, energy_out.at[pl.ds(source * share, share)], e_send.at[i], e_recv.at[i], aux=to_aux(i)
        )

    for i in range(1, groups):
        e_copy(i, row).start()
    energy_out[pl.ds(row * share, share)] = energy_row[...]

    for k in range(CHUNKS):
        done = window if k < CHUNKS - 1 else 0
        loop(
            clusters - 1 - done,
            lambda j, k=k, done=done: slab_copy(k, far_first(j + done), cluster).wait_send(),
        )
    for i in range(1, groups):
        loop(share, lambda q, i=i: inter_copy(i, q, row).wait_send())
        loop(share, lambda q, i=i: part_copy(i, q).wait_send())
        for k in range(HEAD, CHUNKS):
            loop(share, lambda q, i=i, k=k: tail_copy(k, i, q).wait_send())
    for t in range(ITERS):
        loop(clusters - 1, lambda j, t=t: z_copy(t, j + 1, cluster).wait_send())
        for i in range(1, groups):
            loop(share, lambda q, t=t, i=i: split_copy(t, i, q, row).wait_send())
            loop(clusters, lambda j, t=t, i=i: f_copy(t, i, j, from_pair(j), row).wait_send())
    for i in range(1, groups):
        loop(share, lambda q, i=i: out_copy(i, q, row).wait_send())
        loop(share, lambda q, i=i: out_copy(i, q, from_aux(i)).wait_recv())
        e_copy(i, row).wait_send()
        e_copy(i, from_aux(i)).wait_recv()
    out_own.wait()


def on_device(
    orbital_slabs, pno_maps, intersections, pno_energy, occ_energy, pair_orbitals, partners, live
):
    clusters = lax.axis_size("pair")
    groups = lax.axis_size("aux")
    _, aux_rows, virt = orbital_slabs.shape
    pair_count, _, width = pno_maps.shape
    cols = intersections.shape[1]
    share = pair_count // groups
    unit = aux_rows // sum(PARTS)
    head_rows = sum(PARTS[:HEAD]) * unit
    tails = [2 * part * unit for part in PARTS[HEAD:]]
    piece = width // groups
    square = (width, width)
    vm = pltpu.VMEM
    dma = lambda *shape: pltpu.SemaphoreType.DMA(shape)
    scratch = (
        [vm((clusters, part * unit, virt), BF16) for part in PARTS] * 2
        + [vm((groups - 1, share, rows, width), BF16) for rows in tails]
        + [vm((groups, share, rows, width), BF16) for rows in tails]
        + [
            pltpu.SMEM((2 * clusters,), jnp.int32),
            vm((pair_count, virt, width), BF16),
            vm((groups, share, cols) + square, BF16),
            vm((pair_count, head_rows, width), BF16),
            vm((pair_count, head_rows, width), BF16),
            vm((groups - 1, share) + square, BF16),
            vm((groups - 1, share) + square, BF16),
            vm((share,) + square, F32),
            vm((share,) + square, BF16),
            vm((share,) + square, F32),
            vm((share,) + square, F32),
            vm((share,) + square, F32),
            vm((share,) + square, BF16),
            vm((share, 1, width), F32),
        ]
        + [vm((groups, share, piece, width), BF16)] * ITERS
        + [vm((pair_count, piece, width), BF16)] * ITERS
        + [vm((clusters, piece, width), BF16)] * (2 * ITERS)
        + [vm((clusters, groups, piece, width), BF16)]
        + [
            dma(3), dma(groups, share), dma(groups, share), dma(CHUNKS, clusters), dma(CHUNKS, clusters),
            dma(groups, share), dma(groups, share), dma(CHUNKS - HEAD, groups, share),
            dma(CHUNKS - HEAD, groups, share), dma(ITERS, groups, share), dma(ITERS, groups, share),
            dma(ITERS, clusters), dma(ITERS, clusters), dma(ITERS, groups, clusters),
            dma(ITERS, groups, clusters), dma(groups, share), dma(groups, share), dma(groups),
            dma(groups),
        ]
    )
    smem = pl.BlockSpec(memory_space=pltpu.SMEM)
    vmem = pl.BlockSpec(memory_space=pltpu.VMEM)
    anywhere = pl.BlockSpec(memory_space=pl.ANY)
    result, energy = pl.pallas_call(
        functools.partial(kernel, groups, clusters),
        out_shape=(
            jax.ShapeDtypeStruct((pair_count,) + square, BF16),
            jax.ShapeDtypeStruct((pair_count, 1, width), F32),
        ),
        in_specs=[smem] * 4 + [vmem, vmem, anywhere, anywhere],
        out_specs=(anywhere, vmem),
        scratch_shapes=scratch,
        compiler_params=pltpu.CompilerParams(
            collective_id=0, has_side_effects=True, vmem_limit_bytes=62 << 20
        ),
        name="local_pair_amplitudes",
    )(
        pair_orbitals.T, partners.T, live, occ_energy, orbital_slabs, pno_energy, pno_maps,
        intersections,
    )
    return result, jnp.sum(energy, axis=(1, 2))


def solution(mesh):
    placed = (
        P("pair", "aux", None),
        P("pair", None, None),
        P("pair", "aux", None, None),
        P("pair", None),
        P(),
        P(),
        P(),
        P("pair"),
    )
    return jax.shard_map(
        on_device,
        mesh=mesh,
        in_specs=placed,
        out_specs=(P("pair", None, None), P("pair")),
        check_vma=False,
    )
```

```python
import functools

import jax
import jax.numpy as jnp
from jax import lax
from jax.experimental import pallas as pl
from jax.experimental.pallas import tpu as pltpu
from jax.sharding import PartitionSpec as P

ITERS = 2
PARTS = (6, 6, 4)
CHUNKS = len(PARTS)
HEAD = 2
damping = 0.7
BF16 = jnp.bfloat16
F32 = jnp.float32


def dot(x, y, dims):
    return lax.dot_general(x, y, ((dims[:1], dims[1:]), ((), ())), preferred_element_type=F32)


def kernel(
    groups, clusters, orbitals, refs, live, occ, slab, energy, maps_hbm, inter_hbm,
    out_hbm, energy_out, *scratch
):
    scratch = list(scratch)

    def take(count):
        got = scratch[:count]
        del scratch[:count]
        return got

    staged, incoming = take(CHUNKS), take(CHUNKS)
    tail_out, tail_in = take(CHUNKS - HEAD), take(CHUNKS - HEAD)
    (table, maps, inter, left, right, part_out, part_in, coulomb, coulomb_half, denom, rden) = take(11)
    (amp, half, energy_row) = take(3)
    split, quarter, zout, zin = (take(ITERS) for _ in range(4))
    (fetched,) = take(1)
    (
        maps_sem, inter_send, inter_recv, slab_send, slab_recv, part_send, part_recv, tail_send, tail_recv, split_send,
        split_recv, z_send, z_recv, f_send, f_recv, out_send, out_recv, pass_send, pass_recv, e_send, e_recv,
    ) = scratch

    row = lax.axis_index("aux")
    cluster = lax.axis_index("pair")
    pair_count, virt, width = maps.shape
    share = pair_count // groups
    orb_count = slab.shape[0]
    local_cols = inter.shape[2]
    ref_cols = groups * local_cols
    unit = slab.shape[1] // sum(PARTS)
    starts = [sum(PARTS[:k]) * unit for k in range(CHUNKS + 1)]
    piece = width // groups

    def remote(src, dst, send, recv, **where):
        return pltpu.make_async_remote_copy(
            src_ref=src, dst_ref=dst, send_sem=send, recv_sem=recv, device_id=where,
            device_id_type=pl.DeviceIdType.MESH,
        )

    def loop(count, body):
        def step(i, carry):
            body(i)
            return carry

        lax.fori_loop(0, count, step, 0)

    def to_pair(i):
        return lax.rem(cluster + i, clusters)

    def from_pair(i):
        return lax.rem(cluster + clusters - i, clusters)

    def to_aux(i):
        return lax.rem(row + i, groups)

    def from_aux(i):
        return lax.rem(row + groups - i, groups)

    def far_first(j):
        return lax.rem(clusters // 2 - 1 + j, clusters - 1) + 1

    barrier = pltpu.get_barrier_semaphore()
    for i in range(1, clusters):
        pl.semaphore_signal(
            barrier, inc=1, device_id={"pair": to_pair(i)}, device_id_type=pl.DeviceIdType.MESH
        )
    for i in range(1, groups):
        pl.semaphore_signal(
            barrier, inc=1, device_id={"aux": to_aux(i)}, device_id_type=pl.DeviceIdType.MESH
        )
    maps_copy = pltpu.make_async_copy(maps_hbm, maps, maps_sem.at[0])
    maps_copy.start()
    inter_own = pltpu.make_async_copy(
        inter_hbm.at[pl.ds(row * share, share)], inter.at[row], maps_sem.at[1]
    )
    inter_own.start()

    def scan_orbitals(c):
        found = 0
        for n in range(pair_count):
            for side in range(2):
                at = orbitals[side, c * pair_count + n] - cluster * orb_count
                found = jnp.where((at >= 0) & (at < orb_count), at, found)
        table[c] = found

    def scan_pairs(c):
        found = 0
        for n in range(pair_count):
            for r in range(ref_cols):
                at = refs[r, c * pair_count + n] - cluster * pair_count
                found = jnp.where((at >= 0) & (at < pair_count), at, found)
        table[clusters + c] = found

    loop(clusters, scan_orbitals)
    pl.semaphore_wait(barrier, clusters + groups - 2)

    def slab_copy(k, i, source):
        return remote(
            staged[k].at[to_pair(i)], incoming[k].at[source], slab_send.at[k, i],
            slab_recv.at[k, i], pair=to_pair(i),
        )

    def inter_copy(i, source):
        return remote(
            inter_hbm.at[pl.ds(to_aux(i) * share, share)], inter.at[source], inter_send.at[i],
            inter_recv.at[i], aux=to_aux(i),
        )

    for k in range(CHUNKS):
        rows = slice(starts[k], starts[k + 1])

        def send_slab(j, k=k, rows=rows):
            i = far_first(j)
            to = to_pair(i)
            staged[k][to] = slab[table[to], rows, :]
            slab_copy(k, i, cluster).start()

        loop(clusters - 1, send_slab)
        incoming[k][cluster] = slab[table[cluster], rows, :]
        if k == 0:
            for i in range(1, groups):
                inter_copy(i, row).start()

    def denominators(q):
        p = cluster * pair_count + row * share + q
        occupied = occ[orbitals[0, p]] + occ[orbitals[1, p]]
        across = jnp.broadcast_to(energy[pl.ds(row * share + q, 1), :], (width, width))
        value = across + across.T - occupied
        denom[q] = value
        rden[q] = 1.0 / value

    loop(share, denominators)
    loop(clusters, scan_pairs)
    maps_copy.wait()

    def project(k, p):
        first = orbitals[0, cluster * pair_count + p] // orb_count
        second = orbitals[1, cluster * pair_count + p] // orb_count
        both = jnp.concatenate([incoming[k][first], incoming[k][second]], axis=0)
        return dot(both, maps[p], (1, 0)).astype(BF16)

    def project_head(k, p):
        both = project(k, p)
        count = starts[k + 1] - starts[k]
        left[p, starts[k]:starts[k + 1], :] = both[:count]
        right[p, starts[k]:starts[k + 1], :] = both[count:]

    def part_copy(i, q):
        return remote(
            part_out.at[i - 1, q], part_in.at[i - 1, q], part_send.at[i, q], part_recv.at[i, q],
            aux=to_aux(i),
        )

    def tail_copy(k, i, q):
        return remote(
            tail_out[k - HEAD].at[i - 1, q], tail_in[k - HEAD].at[i, q],
            tail_send.at[k - HEAD, i, q], tail_recv.at[k - HEAD, i, q], aux=to_aux(i),
        )

    def send_part(q):
        for i in range(groups):
            project_head(HEAD - 1, to_aux(i) * share + q)
        parts = []
        for i in range(groups):
            p = to_aux(i) * share + q
            parts.append(dot(left[p], right[p], (0, 0)))
        coulomb[q] = parts[0]
        for i in range(1, groups):
            part_out[i - 1, q] = parts[i].astype(BF16)
        for i in range(1, groups):
            part_copy(i, q).start()

    def send_tail(k, q):
        parts = [project(k, to_aux(i) * share + q) for i in range(groups)]
        tail_in[k - HEAD][0, q] = parts[0]
        for i in range(1, groups):
            tail_out[k - HEAD][i - 1, q] = parts[i]
        for i in range(1, groups):
            tail_copy(k, i, q).start()

    for k in range(CHUNKS):
        loop(clusters - 1, lambda j, k=k: slab_copy(k, far_first(j), from_pair(far_first(j))).wait_recv())
        if k < HEAD - 1:
            loop(pair_count, lambda p, k=k: project_head(k, p))
        elif k == HEAD - 1:
            loop(share, send_part)
        else:
            loop(share, lambda q, k=k: send_tail(k, q))

    def split_copy(t, i, q, source):
        return remote(
            split[t].at[to_aux(i), q], quarter[t].at[source * share + q],
            split_send.at[t, i, q], split_recv.at[t, i, q], aux=to_aux(i),
        )

    def z_copy(t, i, source):
        return remote(
            zout[t].at[to_pair(i)], zin[t].at[source], z_send.at[t, i], z_recv.at[t, i],
            pair=to_pair(i),
        )

    def f_copy(t, i, j, member, source):
        return remote(
            zin[t].at[member], fetched.at[member, source], f_send.at[t, i, j],
            f_recv.at[t, i, j], aux=to_aux(i),
        )

    def weight(q):
        return live[row * share + q].astype(F32)

    def set_half(t, q, value):
        rounded = value.astype(BF16)
        half[q] = rounded
        for b in range(groups):
            split[t][b, q] = rounded[b * piece:(b + 1) * piece]
        for i in range(1, groups):
            split_copy(t, i, q, row).start()
        quarter[t][row * share + q] = split[t][row, q]

    def start_amplitude(q):
        for i in range(1, groups):
            part_copy(i, q).wait_recv()
        total = coulomb[q]
        for i in range(1, groups):
            total = total + part_in[i - 1, q].astype(F32)
        lefts, rights = [], []
        for k in range(HEAD, CHUNKS):
            count = starts[k + 1] - starts[k]
            for i in range(groups):
                if i:
                    tail_copy(k, i, q).wait_recv()
                lefts.append(tail_in[k - HEAD][i, q, :count, :])
                rights.append(tail_in[k - HEAD][i, q, count:, :])
        total = total + dot(jnp.concatenate(lefts, 0), jnp.concatenate(rights, 0), (0, 0))
        coulomb[q] = total
        coulomb_half[q] = total.astype(BF16)
        value = -weight(q) * total * rden[q]
        amp[q] = value
        set_half(0, q, value)

    loop(share, start_amplitude)

    if groups == 4:
        near = (row + 1 - 2 * lax.rem(row, 2), lax.rem(row + 2, 4))
    else:
        near = tuple(to_aux(i) for i in range(1, groups))
    senders = near if groups == 4 else tuple(from_aux(i) for i in range(1, groups))

    def out_copy(n, q, source):
        return remote(
            half.at[q], out_hbm.at[source * share + q], out_send.at[n, q], out_recv.at[n, q],
            aux=near[n],
        )

    def pass_copy(n, q, source):
        piece_of = out_hbm.at[source * share + q, pl.ds(n * (width // 2), width // 2), :]
        return remote(
            piece_of, piece_of, pass_send.at[n, q], pass_recv.at[n, q], aux=near[1 - n]
        )

    for t in range(ITERS):
        def quadratic(q):
            product = dot(half[q], coulomb_half[q], (1, 1)).astype(BF16)
            settled = dot(product, half[q], (1, 0)) * (1.0 / width)
            before = amp[q]
            residual = coulomb[q] + denom[q] * before + settled
            amp[q] = before - damping * residual * rden[q]

        for i in range(1, groups):
            loop(share, lambda q, t=t, i=i: split_copy(t, i, q, from_aux(i)).wait_recv())

        def send_z(j, t=t):
            i = far_first(j)
            to = to_pair(i)
            zout[t][to] = quarter[t][table[clusters + to]]
            z_copy(t, i, cluster).start()

        loop(clusters - 1, send_z)
        mine = quarter[t][table[clusters + cluster]]
        zin[t][cluster] = mine
        fetched[cluster, row] = mine
        for i in range(1, groups):
            f_copy(t, i, 0, cluster, row).start()
        loop(share, quadratic)

        def forward(j, t=t):
            j = j + 1
            member = from_pair(j)
            z_copy(t, j, member).wait_recv()
            for i in range(1, groups):
                f_copy(t, i, j, member, row).start()
            fetched[member, row] = zin[t][member]

        loop(clusters - 1, forward)
        if t == 0:
            inter_own.wait()
            for i in range(1, groups):
                inter_copy(i, from_aux(i)).wait_recv()

        def arrive(j, t=t):
            for i in range(1, groups):
                f_copy(t, i, j, from_pair(j), from_aux(i)).wait_recv()

        loop(clusters, arrive)

        def update(q, t=t):
            p = cluster * pair_count + row * share + q
            rotated = []
            for r in range(ref_cols):
                partner = fetched[refs[r, p] // pair_count].reshape(width, width)
                overlap = inter[r // local_cols, q, r % local_cols]
                rotated.append(dot(overlap, partner, (1, 0)).astype(BF16))
            coupled = jnp.zeros((width, width), F32)
            for r in range(ref_cols):
                overlap = inter[r // local_cols, q, r % local_cols]
                coupled = coupled + dot(rotated[r], overlap, (1, 1))
            value = amp[q] + damping * coupled * rden[q]
            value = weight(q) * value
            if t < ITERS - 1:
                amp[q] = value
                set_half(t + 1, q, value)
            else:
                half[q] = value.astype(BF16)
                for n in range(len(near)):
                    out_copy(n, q, row).start()
                total = jnp.sum(coulomb[q] * value, axis=0, keepdims=True)
                energy_row[q] = total

        loop(share, update)

    out_own = pltpu.make_async_copy(half, out_hbm.at[pl.ds(row * share, share)], maps_sem.at[2])
    out_own.start()

    def e_copy(i, source):
        return remote(
            energy_row, energy_out.at[pl.ds(source * share, share)], e_send.at[i], e_recv.at[i], aux=to_aux(i)
        )

    for i in range(1, groups):
        e_copy(i, row).start()
    energy_out[pl.ds(row * share, share)] = energy_row[...]

    for n in range(len(near)):

        def passing(q, n=n):
            out_copy(n, q, senders[n]).wait_recv()
            if groups == 4:
                pass_copy(n, q, near[n]).start()

        loop(share, passing)

    for k in range(CHUNKS):
        loop(clusters - 1, lambda j, k=k: slab_copy(k, j + 1, cluster).wait_send())
    for i in range(1, groups):
        inter_copy(i, row).wait_send()
        loop(share, lambda q, i=i: part_copy(i, q).wait_send())
        for k in range(HEAD, CHUNKS):
            loop(share, lambda q, i=i, k=k: tail_copy(k, i, q).wait_send())
    for t in range(ITERS):
        loop(clusters - 1, lambda j, t=t: z_copy(t, j + 1, cluster).wait_send())
        for i in range(1, groups):
            loop(share, lambda q, t=t, i=i: split_copy(t, i, q, row).wait_send())
            loop(clusters, lambda j, t=t, i=i: f_copy(t, i, j, from_pair(j), row).wait_send())
    for i in range(1, groups):
        e_copy(i, row).wait_send()
        e_copy(i, from_aux(i)).wait_recv()
    out_own.wait()
    for n in range(len(near)):
        loop(share, lambda q, n=n: out_copy(n, q, row).wait_send())
        if groups == 4:
            loop(share, lambda q, n=n: pass_copy(n, q, near[n]).wait_send())
            loop(share, lambda q, n=n: pass_copy(n, q, 3 - row).wait_recv())


def on_device(
    orbital_slabs, pno_maps, intersections, pno_energy, occ_energy, pair_orbitals, partners, live
):
    clusters = lax.axis_size("pair")
    groups = lax.axis_size("aux")
    _, aux_rows, virt = orbital_slabs.shape
    pair_count, _, width = pno_maps.shape
    cols = intersections.shape[1]
    share = pair_count // groups
    unit = aux_rows // sum(PARTS)
    head_rows = sum(PARTS[:HEAD]) * unit
    tails = [2 * part * unit for part in PARTS[HEAD:]]
    piece = width // groups
    square = (width, width)
    vm = pltpu.VMEM
    dma = lambda *shape: pltpu.SemaphoreType.DMA(shape)
    scratch = (
        [vm((clusters, part * unit, virt), BF16) for part in PARTS] * 2
        + [vm((groups - 1, share, rows, width), BF16) for rows in tails]
        + [vm((groups, share, rows, width), BF16) for rows in tails]
        + [
            pltpu.SMEM((2 * clusters,), jnp.int32),
            vm((pair_count, virt, width), BF16),
            vm((groups, share, cols) + square, BF16),
            vm((pair_count, head_rows, width), BF16),
            vm((pair_count, head_rows, width), BF16),
            vm((groups - 1, share) + square, BF16),
            vm((groups - 1, share) + square, BF16),
            vm((share,) + square, F32),
            vm((share,) + square, BF16),
            vm((share,) + square, F32),
            vm((share,) + square, F32),
            vm((share,) + square, F32),
            vm((share,) + square, BF16),
            vm((share, 1, width), F32),
        ]
        + [vm((groups, share, piece, width), BF16)] * ITERS
        + [vm((pair_count, piece, width), BF16)] * ITERS
        + [vm((clusters, piece, width), BF16)] * (2 * ITERS)
        + [vm((clusters, groups, piece, width), BF16)]
        + [
            dma(3), dma(groups), dma(groups), dma(CHUNKS, clusters), dma(CHUNKS, clusters),
            dma(groups, share), dma(groups, share), dma(CHUNKS - HEAD, groups, share),
            dma(CHUNKS - HEAD, groups, share), dma(ITERS, groups, share), dma(ITERS, groups, share),
            dma(ITERS, clusters), dma(ITERS, clusters), dma(ITERS, groups, clusters),
            dma(ITERS, groups, clusters), dma(groups, share), dma(groups, share), dma(groups, share),
            dma(groups, share), dma(groups),
            dma(groups),
        ]
    )
    smem = pl.BlockSpec(memory_space=pltpu.SMEM)
    vmem = pl.BlockSpec(memory_space=pltpu.VMEM)
    anywhere = pl.BlockSpec(memory_space=pl.ANY)
    result, energy = pl.pallas_call(
        functools.partial(kernel, groups, clusters),
        out_shape=(
            jax.ShapeDtypeStruct((pair_count,) + square, BF16),
            jax.ShapeDtypeStruct((pair_count, 1, width), F32),
        ),
        in_specs=[smem] * 4 + [vmem, vmem, anywhere, anywhere],
        out_specs=(anywhere, vmem),
        scratch_shapes=scratch,
        compiler_params=pltpu.CompilerParams(
            collective_id=0, has_side_effects=True, vmem_limit_bytes=62 << 20
        ),
        name="local_pair_amplitudes",
    )(
        pair_orbitals.T, partners.T, live, occ_energy, orbital_slabs, pno_energy, pno_maps,
        intersections,
    )
    return result, jnp.sum(energy, axis=(1, 2))


def solution(mesh):
    placed = (
        P("pair", "aux", None),
        P("pair", None, None),
        P("pair", "aux", None, None),
        P("pair", None),
        P(),
        P(),
        P(),
        P("pair"),
    )
    return jax.shard_map(
        on_device,
        mesh=mesh,
        in_specs=placed,
        out_specs=(P("pair", None, None), P("pair")),
        check_vma=False,
    )
```

```python
import functools

import jax
import jax.numpy as jnp
from jax import lax
from jax.experimental import pallas as pl
from jax.experimental.pallas import tpu as pltpu
from jax.sharding import PartitionSpec as P

ITERS = 2
PARTS = (5, 5, 4, 2)
CHUNKS = len(PARTS)
HEAD = 2
damping = 0.7
BF16 = jnp.bfloat16
F32 = jnp.float32


def dot(x, y, dims):
    return lax.dot_general(x, y, ((dims[:1], dims[1:]), ((), ())), preferred_element_type=F32)


def kernel(
    groups, clusters, orbitals, refs, live, occ, slab, energy, maps_hbm, inter_hbm,
    out_hbm, energy_out, *scratch
):
    scratch = list(scratch)

    def take(count):
        got = scratch[:count]
        del scratch[:count]
        return got

    staged, incoming = take(CHUNKS), take(CHUNKS)
    tail_out, tail_in = take(CHUNKS - HEAD), take(CHUNKS - HEAD)
    (table, maps, inter, left, right, part_out, part_in, coulomb, coulomb_half, denom, rden) = take(11)
    (amp, half, energy_row) = take(3)
    split, quarter, zout, zin = (take(ITERS) for _ in range(4))
    (fetched,) = take(1)
    (
        maps_sem, inter_send, inter_recv, slab_send, slab_recv, part_send, part_recv, tail_send, tail_recv, split_send,
        split_recv, z_send, z_recv, f_send, f_recv, out_send, out_recv, pass_send, pass_recv, e_send, e_recv,
    ) = scratch

    row = lax.axis_index("aux")
    cluster = lax.axis_index("pair")
    pair_count, virt, width = maps.shape
    share = pair_count // groups
    orb_count = slab.shape[0]
    local_cols = inter.shape[2]
    ref_cols = groups * local_cols
    unit = slab.shape[1] // sum(PARTS)
    starts = [sum(PARTS[:k]) * unit for k in range(CHUNKS + 1)]
    piece = width // groups

    def remote(src, dst, send, recv, **where):
        return pltpu.make_async_remote_copy(
            src_ref=src, dst_ref=dst, send_sem=send, recv_sem=recv, device_id=where,
            device_id_type=pl.DeviceIdType.MESH,
        )

    def loop(count, body):
        def step(i, carry):
            body(i)
            return carry

        lax.fori_loop(0, count, step, 0)

    def to_pair(i):
        return lax.rem(cluster + i, clusters)

    def from_pair(i):
        return lax.rem(cluster + clusters - i, clusters)

    def to_aux(i):
        return lax.rem(row + i, groups)

    def from_aux(i):
        return lax.rem(row + groups - i, groups)

    def far_first(j):
        return lax.rem(clusters // 2 - 1 + j, clusters - 1) + 1

    barrier = pltpu.get_barrier_semaphore()
    for i in range(1, clusters):
        pl.semaphore_signal(
            barrier, inc=1, device_id={"pair": to_pair(i)}, device_id_type=pl.DeviceIdType.MESH
        )
    for i in range(1, groups):
        pl.semaphore_signal(
            barrier, inc=1, device_id={"aux": to_aux(i)}, device_id_type=pl.DeviceIdType.MESH
        )
    maps_copy = pltpu.make_async_copy(maps_hbm, maps, maps_sem.at[0])
    maps_copy.start()
    inter_own = pltpu.make_async_copy(
        inter_hbm.at[pl.ds(row * share, share)], inter.at[row], maps_sem.at[1]
    )
    inter_own.start()

    def scan_orbitals(c):
        found = 0
        for n in range(pair_count):
            for side in range(2):
                at = orbitals[side, c * pair_count + n] - cluster * orb_count
                found = jnp.where((at >= 0) & (at < orb_count), at, found)
        table[c] = found

    def scan_pairs(c):
        found = 0
        for n in range(pair_count):
            for r in range(ref_cols):
                at = refs[r, c * pair_count + n] - cluster * pair_count
                found = jnp.where((at >= 0) & (at < pair_count), at, found)
        table[clusters + c] = found

    loop(clusters, scan_orbitals)
    pl.semaphore_wait(barrier, clusters + groups - 2)

    def slab_copy(k, i, source):
        return remote(
            staged[k].at[to_pair(i)], incoming[k].at[source], slab_send.at[k, i],
            slab_recv.at[k, i], pair=to_pair(i),
        )

    def inter_copy(i, source):
        return remote(
            inter_hbm.at[pl.ds(to_aux(i) * share, share)], inter.at[source], inter_send.at[i],
            inter_recv.at[i], aux=to_aux(i),
        )

    for k in range(CHUNKS):
        rows = slice(starts[k], starts[k + 1])

        def send_slab(j, k=k, rows=rows):
            i = far_first(j)
            to = to_pair(i)
            staged[k][to] = slab[table[to], rows, :]
            slab_copy(k, i, cluster).start()

        loop(clusters - 1, send_slab)
        incoming[k][cluster] = slab[table[cluster], rows, :]
        if k == 0:
            for i in range(1, groups):
                inter_copy(i, row).start()

    def denominators(q):
        p = cluster * pair_count + row * share + q
        occupied = occ[orbitals[0, p]] + occ[orbitals[1, p]]
        across = jnp.broadcast_to(energy[pl.ds(row * share + q, 1), :], (width, width))
        value = across + across.T - occupied
        denom[q] = value
        rden[q] = 1.0 / value

    loop(share, denominators)
    loop(clusters, scan_pairs)
    maps_copy.wait()

    def project(k, p):
        first = orbitals[0, cluster * pair_count + p] // orb_count
        second = orbitals[1, cluster * pair_count + p] // orb_count
        both = jnp.concatenate([incoming[k][first], incoming[k][second]], axis=0)
        return dot(both, maps[p], (1, 0)).astype(BF16)

    def project_head(k, p):
        both = project(k, p)
        count = starts[k + 1] - starts[k]
        left[p, starts[k]:starts[k + 1], :] = both[:count]
        right[p, starts[k]:starts[k + 1], :] = both[count:]

    def part_copy(i, q):
        return remote(
            part_out.at[i - 1, q], part_in.at[i - 1, q], part_send.at[i, q], part_recv.at[i, q],
            aux=to_aux(i),
        )

    def tail_copy(k, i, q):
        return remote(
            tail_out[k - HEAD].at[i - 1, q], tail_in[k - HEAD].at[i, q],
            tail_send.at[k - HEAD, i, q], tail_recv.at[k - HEAD, i, q], aux=to_aux(i),
        )

    def send_part(q):
        for i in range(groups):
            project_head(HEAD - 1, to_aux(i) * share + q)
        parts = []
        for i in range(groups):
            p = to_aux(i) * share + q
            parts.append(dot(left[p], right[p], (0, 0)))
        coulomb[q] = parts[0]
        for i in range(1, groups):
            part_out[i - 1, q] = parts[i].astype(BF16)
        for i in range(1, groups):
            part_copy(i, q).start()

    def send_tail(k, q):
        parts = [project(k, to_aux(i) * share + q) for i in range(groups)]
        tail_in[k - HEAD][0, q] = parts[0]
        for i in range(1, groups):
            tail_out[k - HEAD][i - 1, q] = parts[i]
        for i in range(1, groups):
            tail_copy(k, i, q).start()

    for k in range(CHUNKS):
        loop(clusters - 1, lambda j, k=k: slab_copy(k, far_first(j), from_pair(far_first(j))).wait_recv())
        if k < HEAD - 1:
            loop(pair_count, lambda p, k=k: project_head(k, p))
        elif k == HEAD - 1:
            loop(share, send_part)
        else:
            loop(share, lambda q, k=k: send_tail(k, q))

    def split_copy(t, i, q, source):
        return remote(
            split[t].at[to_aux(i), q], quarter[t].at[source * share + q],
            split_send.at[t, i, q], split_recv.at[t, i, q], aux=to_aux(i),
        )

    def z_copy(t, i, source):
        return remote(
            zout[t].at[to_pair(i)], zin[t].at[source], z_send.at[t, i], z_recv.at[t, i],
            pair=to_pair(i),
        )

    def f_copy(t, i, j, member, source):
        return remote(
            zin[t].at[member], fetched.at[member, source], f_send.at[t, i, j],
            f_recv.at[t, i, j], aux=to_aux(i),
        )

    def weight(q):
        return live[row * share + q].astype(F32)

    def set_half(t, q, value):
        rounded = value.astype(BF16)
        half[q] = rounded
        for b in range(groups):
            split[t][b, q] = rounded[b * piece:(b + 1) * piece]
        for i in range(1, groups):
            split_copy(t, i, q, row).start()
        quarter[t][row * share + q] = split[t][row, q]

    def start_amplitude(q):
        total = coulomb[q]
        lefts, rights = [], []
        for k in range(HEAD, CHUNKS):
            count = starts[k + 1] - starts[k]
            for i in range(groups):
                if i:
                    tail_copy(k, i, q).wait_recv()
                lefts.append(tail_in[k - HEAD][i, q, :count, :])
                rights.append(tail_in[k - HEAD][i, q, count:, :])
        total = total + dot(jnp.concatenate(lefts, 0), jnp.concatenate(rights, 0), (0, 0))
        coulomb[q] = total
        coulomb_half[q] = total.astype(BF16)
        value = -weight(q) * total * rden[q]
        amp[q] = value
        set_half(0, q, value)

    def add_parts(q):
        for i in range(1, groups):
            part_copy(i, q).wait_recv()
        total = coulomb[q]
        for i in range(1, groups):
            total = total + part_in[i - 1, q].astype(F32)
        coulomb[q] = total

    loop(share, add_parts)
    loop(share, start_amplitude)

    if groups == 4:
        near = (row + 1 - 2 * lax.rem(row, 2), lax.rem(row + 2, 4))
    else:
        near = tuple(to_aux(i) for i in range(1, groups))
    senders = near if groups == 4 else tuple(from_aux(i) for i in range(1, groups))

    def out_copy(n, q, source):
        return remote(
            half.at[q], out_hbm.at[source * share + q], out_send.at[n, q], out_recv.at[n, q],
            aux=near[n],
        )

    def pass_copy(n, q, source):
        piece_of = out_hbm.at[source * share + q, pl.ds(n * (width // 2), width // 2), :]
        return remote(
            piece_of, piece_of, pass_send.at[n, q], pass_recv.at[n, q], aux=near[1 - n]
        )

    for t in range(ITERS):
        def quadratic(q):
            product = dot(half[q], coulomb_half[q], (1, 1)).astype(BF16)
            settled = dot(product, half[q], (1, 0)) * (1.0 / width)
            before = amp[q]
            residual = coulomb[q] + denom[q] * before + settled
            amp[q] = before - damping * residual * rden[q]

        for i in range(1, groups):
            loop(share, lambda q, t=t, i=i: split_copy(t, i, q, from_aux(i)).wait_recv())

        def send_z(j, t=t):
            i = far_first(j)
            to = to_pair(i)
            zout[t][to] = quarter[t][table[clusters + to]]
            z_copy(t, i, cluster).start()

        loop(clusters - 1, send_z)
        mine = quarter[t][table[clusters + cluster]]
        zin[t][cluster] = mine
        fetched[cluster, row] = mine
        for i in range(1, groups):
            f_copy(t, i, 0, cluster, row).start()
        loop(share, quadratic)

        def forward(j, t=t):
            j = j + 1
            member = from_pair(j)
            z_copy(t, j, member).wait_recv()
            for i in range(1, groups):
                f_copy(t, i, j, member, row).start()
            fetched[member, row] = zin[t][member]

        loop(clusters - 1, forward)
        if t == 0:
            inter_own.wait()
            for i in range(1, groups):
                inter_copy(i, from_aux(i)).wait_recv()

        def arrive(j, t=t):
            for i in range(1, groups):
                f_copy(t, i, j, from_pair(j), from_aux(i)).wait_recv()

        loop(clusters, arrive)

        def update(q, t=t):
            p = cluster * pair_count + row * share + q
            rotated = []
            for r in range(ref_cols):
                partner = fetched[refs[r, p] // pair_count].reshape(width, width)
                overlap = inter[r // local_cols, q, r % local_cols]
                rotated.append(dot(overlap, partner, (1, 0)).astype(BF16))
            coupled = jnp.zeros((width, width), F32)
            for r in range(ref_cols):
                overlap = inter[r // local_cols, q, r % local_cols]
                coupled = coupled + dot(rotated[r], overlap, (1, 1))
            value = amp[q] + damping * coupled * rden[q]
            value = weight(q) * value
            if t < ITERS - 1:
                amp[q] = value
                set_half(t + 1, q, value)
            else:
                half[q] = value.astype(BF16)
                for n in range(len(near)):
                    out_copy(n, q, row).start()
                total = jnp.sum(coulomb[q] * value, axis=0, keepdims=True)
                energy_row[q] = total

        loop(share, update)

    out_own = pltpu.make_async_copy(half, out_hbm.at[pl.ds(row * share, share)], maps_sem.at[2])
    out_own.start()

    def e_copy(i, source):
        return remote(
            energy_row, energy_out.at[pl.ds(source * share, share)], e_send.at[i], e_recv.at[i], aux=to_aux(i)
        )

    for i in range(1, groups):
        e_copy(i, row).start()
    energy_out[pl.ds(row * share, share)] = energy_row[...]

    def passing(q):
        for n in range(len(near)):
            out_copy(n, q, senders[n]).wait_recv()
            if groups == 4:
                pass_copy(n, q, near[n]).start()

    loop(share, passing)

    for k in range(CHUNKS):
        loop(clusters - 1, lambda j, k=k: slab_copy(k, j + 1, cluster).wait_send())
    for i in range(1, groups):
        inter_copy(i, row).wait_send()
        loop(share, lambda q, i=i: part_copy(i, q).wait_send())
        for k in range(HEAD, CHUNKS):
            loop(share, lambda q, i=i, k=k: tail_copy(k, i, q).wait_send())
    for t in range(ITERS):
        loop(clusters - 1, lambda j, t=t: z_copy(t, j + 1, cluster).wait_send())
        for i in range(1, groups):
            loop(share, lambda q, t=t, i=i: split_copy(t, i, q, row).wait_send())
            loop(clusters, lambda j, t=t, i=i: f_copy(t, i, j, from_pair(j), row).wait_send())
    for i in range(1, groups):
        e_copy(i, row).wait_send()
        e_copy(i, from_aux(i)).wait_recv()
    out_own.wait()
    for n in range(len(near)):
        loop(share, lambda q, n=n: out_copy(n, q, row).wait_send())
        if groups == 4:
            loop(share, lambda q, n=n: pass_copy(n, q, near[n]).wait_send())
            loop(share, lambda q, n=n: pass_copy(n, q, 3 - row).wait_recv())


def on_device(
    orbital_slabs, pno_maps, intersections, pno_energy, occ_energy, pair_orbitals, partners, live
):
    clusters = lax.axis_size("pair")
    groups = lax.axis_size("aux")
    _, aux_rows, virt = orbital_slabs.shape
    pair_count, _, width = pno_maps.shape
    cols = intersections.shape[1]
    share = pair_count // groups
    unit = aux_rows // sum(PARTS)
    head_rows = sum(PARTS[:HEAD]) * unit
    tails = [2 * part * unit for part in PARTS[HEAD:]]
    piece = width // groups
    square = (width, width)
    vm = pltpu.VMEM
    dma = lambda *shape: pltpu.SemaphoreType.DMA(shape)
    scratch = (
        [vm((clusters, part * unit, virt), BF16) for part in PARTS] * 2
        + [vm((groups - 1, share, rows, width), BF16) for rows in tails]
        + [vm((groups, share, rows, width), BF16) for rows in tails]
        + [
            pltpu.SMEM((2 * clusters,), jnp.int32),
            vm((pair_count, virt, width), BF16),
            vm((groups, share, cols) + square, BF16),
            vm((pair_count, head_rows, width), BF16),
            vm((pair_count, head_rows, width), BF16),
            vm((groups - 1, share) + square, BF16),
            vm((groups - 1, share) + square, BF16),
            vm((share,) + square, F32),
            vm((share,) + square, BF16),
            vm((share,) + square, F32),
            vm((share,) + square, F32),
            vm((share,) + square, F32),
            vm((share,) + square, BF16),
            vm((share, 1, width), F32),
        ]
        + [vm((groups, share, piece, width), BF16)] * ITERS
        + [vm((pair_count, piece, width), BF16)] * ITERS
        + [vm((clusters, piece, width), BF16)] * (2 * ITERS)
        + [vm((clusters, groups, piece, width), BF16)]
        + [
            dma(3), dma(groups), dma(groups), dma(CHUNKS, clusters), dma(CHUNKS, clusters),
            dma(groups, share), dma(groups, share), dma(CHUNKS - HEAD, groups, share),
            dma(CHUNKS - HEAD, groups, share), dma(ITERS, groups, share), dma(ITERS, groups, share),
            dma(ITERS, clusters), dma(ITERS, clusters), dma(ITERS, groups, clusters),
            dma(ITERS, groups, clusters), dma(groups, share), dma(groups, share), dma(groups, share),
            dma(groups, share), dma(groups),
            dma(groups),
        ]
    )
    smem = pl.BlockSpec(memory_space=pltpu.SMEM)
    vmem = pl.BlockSpec(memory_space=pltpu.VMEM)
    anywhere = pl.BlockSpec(memory_space=pl.ANY)
    result, energy = pl.pallas_call(
        functools.partial(kernel, groups, clusters),
        out_shape=(
            jax.ShapeDtypeStruct((pair_count,) + square, BF16),
            jax.ShapeDtypeStruct((pair_count, 1, width), F32),
        ),
        in_specs=[smem] * 4 + [vmem, vmem, anywhere, anywhere],
        out_specs=(anywhere, vmem),
        scratch_shapes=scratch,
        compiler_params=pltpu.CompilerParams(
            collective_id=0, has_side_effects=True, vmem_limit_bytes=62 << 20
        ),
        name="local_pair_amplitudes",
    )(
        pair_orbitals.T, partners.T, live, occ_energy, orbital_slabs, pno_energy, pno_maps,
        intersections,
    )
    return result, jnp.sum(energy, axis=(1, 2))


def solution(mesh):
    placed = (
        P("pair", "aux", None),
        P("pair", None, None),
        P("pair", "aux", None, None),
        P("pair", None),
        P(),
        P(),
        P(),
        P("pair"),
    )
    return jax.shard_map(
        on_device,
        mesh=mesh,
        in_specs=placed,
        out_specs=(P("pair", None, None), P("pair")),
        check_vma=False,
    )
```

```python
import functools

import jax
import jax.numpy as jnp
from jax import lax
from jax.experimental import pallas as pl
from jax.experimental.pallas import tpu as pltpu
from jax.sharding import PartitionSpec as P

ITERS = 2
PARTS = (6, 6, 4)
CHUNKS = len(PARTS)
HEAD = 2
damping = 0.7
BF16 = jnp.bfloat16
F32 = jnp.float32


def dot(x, y, dims):
    return lax.dot_general(x, y, ((dims[:1], dims[1:]), ((), ())), preferred_element_type=F32)


def kernel(
    groups, clusters, orbitals, refs, live, occ, slab, energy, maps_hbm, inter_hbm,
    out_hbm, energy_out, *scratch
):
    scratch = list(scratch)

    def take(count):
        got = scratch[:count]
        del scratch[:count]
        return got

    staged, incoming = take(CHUNKS), take(CHUNKS)
    tail_out, tail_in = take(CHUNKS - HEAD), take(CHUNKS - HEAD)
    (table, maps, inter, left, right, part_out, part_in, coulomb, coulomb_half, denom, rden) = take(11)
    (amp, half, energy_row) = take(3)
    split, quarter, zout, zin = (take(ITERS) for _ in range(4))
    (fetched,) = take(1)
    (
        maps_sem, inter_send, inter_recv, slab_send, slab_recv, part_send, part_recv, tail_send, tail_recv, split_send,
        split_recv, z_send, z_recv, f_send, f_recv, out_send, out_recv, pass_send, pass_recv, e_send, e_recv,
    ) = scratch

    row = lax.axis_index("aux")
    cluster = lax.axis_index("pair")
    pair_count, virt, width = maps.shape
    share = pair_count // groups
    orb_count = slab.shape[0]
    local_cols = inter.shape[2]
    ref_cols = groups * local_cols
    unit = slab.shape[1] // sum(PARTS)
    starts = [sum(PARTS[:k]) * unit for k in range(CHUNKS + 1)]
    piece = width // groups

    def remote(src, dst, send, recv, **where):
        return pltpu.make_async_remote_copy(
            src_ref=src, dst_ref=dst, send_sem=send, recv_sem=recv, device_id=where,
            device_id_type=pl.DeviceIdType.MESH,
        )

    def loop(count, body):
        def step(i, carry):
            body(i)
            return carry

        lax.fori_loop(0, count, step, 0)

    def to_pair(i):
        return lax.rem(cluster + i, clusters)

    def from_pair(i):
        return lax.rem(cluster + clusters - i, clusters)

    def to_aux(i):
        return lax.rem(row + i, groups)

    def from_aux(i):
        return lax.rem(row + groups - i, groups)

    four = groups == 4
    if four:
        near = (row + 1 - 2 * lax.rem(row, 2), lax.rem(row + 2, 4))
        senders = near
    else:
        near = tuple(to_aux(i) for i in range(1, groups))
        senders = tuple(from_aux(i) for i in range(1, groups))
    far = groups - 1 - row
    hops = range(len(near))

    def half_of(ref, n):
        rows = ref.shape[0] // 2
        return ref.at[pl.ds(n * rows, rows), :]

    def far_first(j):
        return lax.rem(clusters // 2 - 1 + j, clusters - 1) + 1

    barrier = pltpu.get_barrier_semaphore()
    for i in range(1, clusters):
        pl.semaphore_signal(
            barrier, inc=1, device_id={"pair": to_pair(i)}, device_id_type=pl.DeviceIdType.MESH
        )
    for i in range(1, groups):
        pl.semaphore_signal(
            barrier, inc=1, device_id={"aux": to_aux(i)}, device_id_type=pl.DeviceIdType.MESH
        )
    maps_copy = pltpu.make_async_copy(maps_hbm, maps, maps_sem.at[0])
    maps_copy.start()
    inter_own = pltpu.make_async_copy(
        inter_hbm.at[pl.ds(row * share, share)], inter.at[row], maps_sem.at[1]
    )
    inter_own.start()

    def scan_orbitals(c):
        found = 0
        for n in range(pair_count):
            for side in range(2):
                at = orbitals[side, c * pair_count + n] - cluster * orb_count
                found = jnp.where((at >= 0) & (at < orb_count), at, found)
        table[c] = found

    def scan_pairs(c):
        found = 0
        for n in range(pair_count):
            for r in range(ref_cols):
                at = refs[r, c * pair_count + n] - cluster * pair_count
                found = jnp.where((at >= 0) & (at < pair_count), at, found)
        table[clusters + c] = found

    loop(clusters, scan_orbitals)
    pl.semaphore_wait(barrier, clusters + groups - 2)

    def slab_copy(k, i, source):
        return remote(
            staged[k].at[to_pair(i)], incoming[k].at[source], slab_send.at[k, i],
            slab_recv.at[k, i], pair=to_pair(i),
        )

    def inter_copy(i, source):
        return remote(
            inter_hbm.at[pl.ds(to_aux(i) * share, share)], inter.at[source], inter_send.at[i],
            inter_recv.at[i], aux=to_aux(i),
        )

    for k in range(CHUNKS):
        rows = slice(starts[k], starts[k + 1])

        def send_slab(j, k=k, rows=rows):
            i = far_first(j)
            to = to_pair(i)
            staged[k][to] = slab[table[to], rows, :]
            slab_copy(k, i, cluster).start()

        loop(clusters - 1, send_slab)
        incoming[k][cluster] = slab[table[cluster], rows, :]
        if k == 0:
            for i in range(1, groups):
                inter_copy(i, row).start()

    def denominators(q):
        p = cluster * pair_count + row * share + q
        occupied = occ[orbitals[0, p]] + occ[orbitals[1, p]]
        across = jnp.broadcast_to(energy[pl.ds(row * share + q, 1), :], (width, width))
        value = across + across.T - occupied
        denom[q] = value
        rden[q] = 1.0 / value

    loop(share, denominators)
    loop(clusters, scan_pairs)
    maps_copy.wait()

    def project(k, p):
        first = orbitals[0, cluster * pair_count + p] // orb_count
        second = orbitals[1, cluster * pair_count + p] // orb_count
        both = jnp.concatenate([incoming[k][first], incoming[k][second]], axis=0)
        return dot(both, maps[p], (1, 0)).astype(BF16)

    def project_head(k, p):
        both = project(k, p)
        count = starts[k + 1] - starts[k]
        left[p, starts[k]:starts[k + 1], :] = both[:count]
        right[p, starts[k]:starts[k + 1], :] = both[count:]

    def part_copy(n, q):
        return remote(
            part_out.at[n, q], part_in.at[n, q], part_send.at[n, q], part_recv.at[n, q],
            aux=near[n],
        )

    def far_copy(n, q):
        return remote(
            half_of(part_out.at[2, q], n), half_of(part_in.at[2, q], n), part_send.at[2 + n, q],
            part_recv.at[2 + n, q], aux=near[n],
        )

    def tail_copy(k, i, q):
        return remote(
            tail_out[k - HEAD].at[i - 1, q], tail_in[k - HEAD].at[i, q],
            tail_send.at[k - HEAD, i, q], tail_recv.at[k - HEAD, i, q], aux=to_aux(i),
        )

    def head_sum(p):
        project_head(HEAD - 1, p)
        return dot(left[p], right[p], (0, 0))

    def send_far(q):
        part_out[2, q] = head_sum(far * share + q).astype(BF16)
        for n in hops:
            far_copy(n, q).start()

    def own_part(q):
        coulomb[q] = head_sum(row * share + q)

    def send_part(q):
        sums = [head_sum(near[n] * share + q) for n in hops]
        for n in hops:
            total = sums[n]
            if four:
                far_copy(1 - n, q).wait_recv()
                rows = width // 2
                passing_by = part_in[2, q, (1 - n) * rows:(2 - n) * rows, :].astype(F32)
                parts = [total[:rows], total[rows:]]
                parts[1 - n] = parts[1 - n] + passing_by
                total = jnp.concatenate(parts, axis=0)
            part_out[n, q] = total.astype(BF16)
        for n in hops:
            part_copy(n, q).start()

    def send_head():
        if four:
            loop(share, send_far)
        loop(share, own_part)
        loop(share, send_part)

    def send_tail(k, q):
        parts = [project(k, to_aux(i) * share + q) for i in range(groups)]
        tail_in[k - HEAD][0, q] = parts[0]
        for i in range(1, groups):
            tail_out[k - HEAD][i - 1, q] = parts[i]
        for i in range(1, groups):
            tail_copy(k, i, q).start()

    for k in range(CHUNKS):
        loop(clusters - 1, lambda j, k=k: slab_copy(k, far_first(j), from_pair(far_first(j))).wait_recv())
        if k < HEAD - 1:
            loop(pair_count, lambda p, k=k: project_head(k, p))
        elif k == HEAD - 1:
            send_head()
        else:
            loop(share, lambda q, k=k: send_tail(k, q))

    def split_copy(t, i, q, source):
        return remote(
            split[t].at[to_aux(i), q], quarter[t].at[source * share + q],
            split_send.at[t, i, q], split_recv.at[t, i, q], aux=to_aux(i),
        )

    def z_copy(t, i, source):
        return remote(
            zout[t].at[to_pair(i)], zin[t].at[source], z_send.at[t, i], z_recv.at[t, i],
            pair=to_pair(i),
        )

    def f_copy(t, n, j, source):
        member = from_pair(j)
        return remote(
            zin[t].at[member], fetched.at[member, source], f_send.at[t, n, j], f_recv.at[t, n, j],
            aux=near[n],
        )

    def f_pass(t, n, j, source):
        piece_of = half_of(fetched.at[from_pair(j), source], n)
        return remote(
            piece_of, piece_of, f_send.at[t, 2 + n, j], f_recv.at[t, 2 + n, j], aux=near[1 - n]
        )

    def weight(q):
        return live[row * share + q].astype(F32)

    def set_half(t, q, value):
        rounded = value.astype(BF16)
        half[q] = rounded
        for b in range(groups):
            split[t][b, q] = rounded[b * piece:(b + 1) * piece]
        for i in range(1, groups):
            split_copy(t, i, q, row).start()
        quarter[t][row * share + q] = split[t][row, q]

    def start_amplitude(q):
        total = coulomb[q]
        lefts, rights = [], []
        for k in range(HEAD, CHUNKS):
            count = starts[k + 1] - starts[k]
            for i in range(groups):
                if i:
                    tail_copy(k, i, q).wait_recv()
                lefts.append(tail_in[k - HEAD][i, q, :count, :])
                rights.append(tail_in[k - HEAD][i, q, count:, :])
        total = total + dot(jnp.concatenate(lefts, 0), jnp.concatenate(rights, 0), (0, 0))
        coulomb[q] = total
        coulomb_half[q] = total.astype(BF16)
        value = -weight(q) * total * rden[q]
        amp[q] = value
        set_half(0, q, value)

    def add_parts(q):
        total = coulomb[q]
        for n in hops:
            part_copy(n, q).wait_recv()
            total = total + part_in[n, q].astype(F32)
        coulomb[q] = total

    loop(share, add_parts)
    loop(share, start_amplitude)

    def out_copy(n, q, source):
        return remote(
            half.at[q], out_hbm.at[source * share + q], out_send.at[n, q], out_recv.at[n, q],
            aux=near[n],
        )

    def pass_copy(n, q, source):
        piece_of = half_of(out_hbm.at[source * share + q], n)
        return remote(
            piece_of, piece_of, pass_send.at[n, q], pass_recv.at[n, q], aux=near[1 - n]
        )

    for t in range(ITERS):
        def quadratic(q):
            product = dot(half[q], coulomb_half[q], (1, 1)).astype(BF16)
            settled = dot(product, half[q], (1, 0)) * (1.0 / width)
            before = amp[q]
            residual = coulomb[q] + denom[q] * before + settled
            amp[q] = before - damping * residual * rden[q]

        for i in range(1, groups):
            loop(share, lambda q, t=t, i=i: split_copy(t, i, q, from_aux(i)).wait_recv())

        def send_z(j, t=t):
            i = far_first(j)
            to = to_pair(i)
            zout[t][to] = quarter[t][table[clusters + to]]
            z_copy(t, i, cluster).start()

        loop(clusters - 1, send_z)
        mine = quarter[t][table[clusters + cluster]]
        zin[t][cluster] = mine
        fetched[cluster, row] = mine
        for n in hops:
            f_copy(t, n, 0, row).start()
        loop(share, quadratic)

        def hand_on(j, t=t):
            for n in hops:
                f_copy(t, n, j, senders[n]).wait_recv()
                if four:
                    f_pass(t, n, j, near[n]).start()

        def forward(j, t=t):
            j = j + 1
            member = from_pair(j)
            z_copy(t, j, member).wait_recv()
            for n in hops:
                f_copy(t, n, j, row).start()
            fetched[member, row] = zin[t][member]
            hand_on(j - 1)

        loop(clusters - 1, forward)
        hand_on(clusters - 1)
        if t == 0:
            inter_own.wait()
            for i in range(1, groups):
                inter_copy(i, from_aux(i)).wait_recv()
        if four:
            for n in hops:
                loop(clusters, lambda j, t=t, n=n: f_pass(t, n, j, far).wait_recv())
                loop(clusters, lambda j, t=t, n=n: f_pass(t, n, j, near[n]).wait_send())

        def update(q, t=t):
            p = cluster * pair_count + row * share + q
            rotated = []
            for r in range(ref_cols):
                partner = fetched[refs[r, p] // pair_count].reshape(width, width)
                overlap = inter[r // local_cols, q, r % local_cols]
                rotated.append(dot(overlap, partner, (1, 0)).astype(BF16))
            coupled = jnp.zeros((width, width), F32)
            for r in range(ref_cols):
                overlap = inter[r // local_cols, q, r % local_cols]
                coupled = coupled + dot(rotated[r], overlap, (1, 1))
            value = amp[q] + damping * coupled * rden[q]
            value = weight(q) * value
            if t < ITERS - 1:
                amp[q] = value
                set_half(t + 1, q, value)
            else:
                half[q] = value.astype(BF16)
                for n in hops:
                    out_copy(n, q, row).start()
                total = jnp.sum(coulomb[q] * value, axis=0, keepdims=True)
                energy_row[q] = total

        loop(share, update)

    out_own = pltpu.make_async_copy(half, out_hbm.at[pl.ds(row * share, share)], maps_sem.at[2])
    out_own.start()

    def e_copy(i, source):
        return remote(
            energy_row, energy_out.at[pl.ds(source * share, share)], e_send.at[i], e_recv.at[i], aux=to_aux(i)
        )

    for i in range(1, groups):
        e_copy(i, row).start()
    energy_out[pl.ds(row * share, share)] = energy_row[...]

    def passing(q):
        for n in hops:
            out_copy(n, q, senders[n]).wait_recv()
            if four:
                pass_copy(n, q, near[n]).start()

    loop(share, passing)

    for k in range(CHUNKS):
        loop(clusters - 1, lambda j, k=k: slab_copy(k, j + 1, cluster).wait_send())
    for i in range(1, groups):
        inter_copy(i, row).wait_send()
        for k in range(HEAD, CHUNKS):
            loop(share, lambda q, i=i, k=k: tail_copy(k, i, q).wait_send())
    for t in range(ITERS):
        loop(clusters - 1, lambda j, t=t: z_copy(t, j + 1, cluster).wait_send())
        for i in range(1, groups):
            loop(share, lambda q, t=t, i=i: split_copy(t, i, q, row).wait_send())
        for n in hops:
            loop(clusters, lambda j, t=t, n=n: f_copy(t, n, j, row).wait_send())
    for i in range(1, groups):
        e_copy(i, row).wait_send()
        e_copy(i, from_aux(i)).wait_recv()
    out_own.wait()
    for n in hops:
        loop(share, lambda q, n=n: part_copy(n, q).wait_send())
        if four:
            loop(share, lambda q, n=n: far_copy(n, q).wait_send())
        loop(share, lambda q, n=n: out_copy(n, q, row).wait_send())
        if four:
            loop(share, lambda q, n=n: pass_copy(n, q, near[n]).wait_send())
            loop(share, lambda q, n=n: pass_copy(n, q, 3 - row).wait_recv())


def on_device(
    orbital_slabs, pno_maps, intersections, pno_energy, occ_energy, pair_orbitals, partners, live
):
    clusters = lax.axis_size("pair")
    groups = lax.axis_size("aux")
    _, aux_rows, virt = orbital_slabs.shape
    pair_count, _, width = pno_maps.shape
    cols = intersections.shape[1]
    share = pair_count // groups
    unit = aux_rows // sum(PARTS)
    head_rows = sum(PARTS[:HEAD]) * unit
    tails = [2 * part * unit for part in PARTS[HEAD:]]
    piece = width // groups
    square = (width, width)
    vm = pltpu.VMEM
    dma = lambda *shape: pltpu.SemaphoreType.DMA(shape)
    scratch = (
        [vm((clusters, part * unit, virt), BF16) for part in PARTS] * 2
        + [vm((groups - 1, share, rows, width), BF16) for rows in tails]
        + [vm((groups, share, rows, width), BF16) for rows in tails]
        + [
            pltpu.SMEM((2 * clusters,), jnp.int32),
            vm((pair_count, virt, width), BF16),
            vm((groups, share, cols) + square, BF16),
            vm((pair_count, head_rows, width), BF16),
            vm((pair_count, head_rows, width), BF16),
            vm((groups - 1, share) + square, BF16),
            vm((groups - 1, share) + square, BF16),
            vm((share,) + square, F32),
            vm((share,) + square, BF16),
            vm((share,) + square, F32),
            vm((share,) + square, F32),
            vm((share,) + square, F32),
            vm((share,) + square, BF16),
            vm((share, 1, width), F32),
        ]
        + [vm((groups, share, piece, width), BF16)] * ITERS
        + [vm((pair_count, piece, width), BF16)] * ITERS
        + [vm((clusters, piece, width), BF16)] * (2 * ITERS)
        + [vm((clusters, groups, piece, width), BF16)]
        + [
            dma(3), dma(groups), dma(groups), dma(CHUNKS, clusters), dma(CHUNKS, clusters),
            dma(groups, share), dma(groups, share), dma(CHUNKS - HEAD, groups, share),
            dma(CHUNKS - HEAD, groups, share), dma(ITERS, groups, share), dma(ITERS, groups, share),
            dma(ITERS, clusters), dma(ITERS, clusters), dma(ITERS, groups, clusters),
            dma(ITERS, groups, clusters), dma(groups, share), dma(groups, share), dma(groups, share),
            dma(groups, share), dma(groups),
            dma(groups),
        ]
    )
    smem = pl.BlockSpec(memory_space=pltpu.SMEM)
    vmem = pl.BlockSpec(memory_space=pltpu.VMEM)
    anywhere = pl.BlockSpec(memory_space=pl.ANY)
    result, energy = pl.pallas_call(
        functools.partial(kernel, groups, clusters),
        out_shape=(
            jax.ShapeDtypeStruct((pair_count,) + square, BF16),
            jax.ShapeDtypeStruct((pair_count, 1, width), F32),
        ),
        in_specs=[smem] * 4 + [vmem, vmem, anywhere, anywhere],
        out_specs=(anywhere, vmem),
        scratch_shapes=scratch,
        compiler_params=pltpu.CompilerParams(
            collective_id=0, has_side_effects=True, vmem_limit_bytes=62 << 20
        ),
        name="local_pair_amplitudes",
    )(
        pair_orbitals.T, partners.T, live, occ_energy, orbital_slabs, pno_energy, pno_maps,
        intersections,
    )
    return result, jnp.sum(energy, axis=(1, 2))


def solution(mesh):
    placed = (
        P("pair", "aux", None),
        P("pair", None, None),
        P("pair", "aux", None, None),
        P("pair", None),
        P(),
        P(),
        P(),
        P("pair"),
    )
    return jax.shard_map(
        on_device,
        mesh=mesh,
        in_specs=placed,
        out_specs=(P("pair", None, None), P("pair")),
        check_vma=False,
    )
```

```python
import functools

import jax
import jax.numpy as jnp
from jax import lax
from jax.experimental import pallas as pl
from jax.experimental.pallas import tpu as pltpu
from jax.sharding import PartitionSpec as P

ITERS = 2
PARTS = (6, 6, 4)
CHUNKS = len(PARTS)
HEAD = 2
damping = 0.7
BF16 = jnp.bfloat16
F32 = jnp.float32


def dot(x, y, dims):
    return lax.dot_general(x, y, ((dims[:1], dims[1:]), ((), ())), preferred_element_type=F32)


def kernel(
    groups, clusters, orbitals, refs, live, occ, slab, energy, maps_hbm, inter_hbm,
    out_hbm, energy_out, *scratch
):
    scratch = list(scratch)

    def take(count):
        got = scratch[:count]
        del scratch[:count]
        return got

    staged, incoming = take(CHUNKS), take(CHUNKS)
    tail_out, tail_in = take(CHUNKS - HEAD), take(CHUNKS - HEAD)
    (table, maps, inter, left, right, part_out, part_in, coulomb, coulomb_half, denom, rden) = take(11)
    (amp, half, energy_row) = take(3)
    split, quarter, zout, zin = (take(ITERS) for _ in range(4))
    (fetched,) = take(1)
    (
        maps_sem, inter_send, inter_recv, slab_send, slab_recv, part_send, part_recv, tail_send, tail_recv, split_send,
        split_recv, z_send, z_recv, f_send, f_recv, out_send, out_recv, pass_send, pass_recv, e_send, e_recv,
    ) = scratch

    row = lax.axis_index("aux")
    cluster = lax.axis_index("pair")
    pair_count, virt, width = maps.shape
    share = pair_count // groups
    orb_count = slab.shape[0]
    local_cols = inter.shape[2]
    ref_cols = groups * local_cols
    unit = slab.shape[1] // sum(PARTS)
    starts = [sum(PARTS[:k]) * unit for k in range(CHUNKS + 1)]
    piece = width // groups

    def remote(src, dst, send, recv, **where):
        return pltpu.make_async_remote_copy(
            src_ref=src, dst_ref=dst, send_sem=send, recv_sem=recv, device_id=where,
            device_id_type=pl.DeviceIdType.MESH,
        )

    def loop(count, body):
        def step(i, carry):
            body(i)
            return carry

        lax.fori_loop(0, count, step, 0)

    def to_pair(i):
        return lax.rem(cluster + i, clusters)

    def from_pair(i):
        return lax.rem(cluster + clusters - i, clusters)

    def to_aux(i):
        return lax.rem(row + i, groups)

    def from_aux(i):
        return lax.rem(row + groups - i, groups)

    four = groups == 4
    if four:
        near = (row + 1 - 2 * lax.rem(row, 2), lax.rem(row + 2, 4))
        senders = near
    else:
        near = tuple(to_aux(i) for i in range(1, groups))
        senders = tuple(from_aux(i) for i in range(1, groups))
    far = groups - 1 - row
    hops = range(len(near))

    def half_of(ref, n):
        rows = ref.shape[0] // 2
        return ref.at[pl.ds(n * rows, rows), :]

    def far_first(j):
        return lax.rem(clusters // 2 - 1 + j, clusters - 1) + 1

    barrier = pltpu.get_barrier_semaphore()
    for i in range(1, clusters):
        pl.semaphore_signal(
            barrier, inc=1, device_id={"pair": to_pair(i)}, device_id_type=pl.DeviceIdType.MESH
        )
    for i in range(1, groups):
        pl.semaphore_signal(
            barrier, inc=1, device_id={"aux": to_aux(i)}, device_id_type=pl.DeviceIdType.MESH
        )
    maps_copy = pltpu.make_async_copy(maps_hbm, maps, maps_sem.at[0])
    maps_copy.start()
    inter_own = pltpu.make_async_copy(
        inter_hbm.at[pl.ds(row * share, share)], inter.at[row], maps_sem.at[1]
    )
    inter_own.start()

    def scan_orbitals(c):
        found = 0
        for n in range(pair_count):
            for side in range(2):
                at = orbitals[side, c * pair_count + n] - cluster * orb_count
                found = jnp.where((at >= 0) & (at < orb_count), at, found)
        table[c] = found

    def scan_pairs(c):
        found = 0
        for n in range(pair_count):
            for r in range(ref_cols):
                at = refs[r, c * pair_count + n] - cluster * pair_count
                found = jnp.where((at >= 0) & (at < pair_count), at, found)
        table[clusters + c] = found

    loop(clusters, scan_orbitals)
    pl.semaphore_wait(barrier, clusters + groups - 2)

    def slab_copy(k, i, source):
        return remote(
            staged[k].at[to_pair(i)], incoming[k].at[source], slab_send.at[k, i],
            slab_recv.at[k, i], pair=to_pair(i),
        )

    def inter_copy(i, q, source):
        return remote(
            inter_hbm.at[to_aux(i) * share + q], inter.at[source, q], inter_send.at[i, q],
            inter_recv.at[i, q], aux=to_aux(i),
        )

    def send_inter(q):
        for i in range(1, groups):
            inter_copy(i, q, row).start()

    mixed = min(share, clusters - 1)
    for k in range(CHUNKS):
        rows = slice(starts[k], starts[k + 1])

        def send_slab(j, k=k, rows=rows):
            i = far_first(j)
            to = to_pair(i)
            staged[k][to] = slab[table[to], rows, :]
            slab_copy(k, i, cluster).start()

        def send_both(j, send_slab=send_slab):
            send_slab(j)
            send_inter(j)

        if k == 0:
            loop(mixed, send_both)
            loop(clusters - 1 - mixed, lambda j, send_slab=send_slab: send_slab(j + mixed))
            loop(share - mixed, lambda q: send_inter(q + mixed))
        else:
            loop(clusters - 1, send_slab)
        incoming[k][cluster] = slab[table[cluster], rows, :]

    def denominators(q):
        p = cluster * pair_count + row * share + q
        occupied = occ[orbitals[0, p]] + occ[orbitals[1, p]]
        across = jnp.broadcast_to(energy[pl.ds(row * share + q, 1), :], (width, width))
        value = across + across.T - occupied
        denom[q] = value
        rden[q] = 1.0 / value

    loop(share, denominators)
    loop(clusters, scan_pairs)
    maps_copy.wait()

    def project(k, p):
        first = orbitals[0, cluster * pair_count + p] // orb_count
        second = orbitals[1, cluster * pair_count + p] // orb_count
        both = jnp.concatenate([incoming[k][first], incoming[k][second]], axis=0)
        return dot(both, maps[p], (1, 0)).astype(BF16)

    def project_head(k, p):
        both = project(k, p)
        count = starts[k + 1] - starts[k]
        left[p, starts[k]:starts[k + 1], :] = both[:count]
        right[p, starts[k]:starts[k + 1], :] = both[count:]

    def part_copy(n, q):
        return remote(
            part_out.at[n, q], part_in.at[n, q], part_send.at[n, q], part_recv.at[n, q],
            aux=near[n],
        )

    def far_copy(n, q):
        return remote(
            half_of(part_out.at[2, q], n), half_of(part_in.at[2, q], n), part_send.at[2 + n, q],
            part_recv.at[2 + n, q], aux=near[n],
        )

    def tail_copy(k, i, q):
        return remote(
            tail_out[k - HEAD].at[i - 1, q], tail_in[k - HEAD].at[i, q],
            tail_send.at[k - HEAD, i, q], tail_recv.at[k - HEAD, i, q], aux=to_aux(i),
        )

    def head_sum(p):
        project_head(HEAD - 1, p)
        return dot(left[p], right[p], (0, 0))

    def send_far(q):
        part_out[2, q] = head_sum(far * share + q).astype(BF16)
        for n in hops:
            far_copy(n, q).start()

    def own_part(q):
        coulomb[q] = head_sum(row * share + q)

    def send_part(q):
        sums = [head_sum(near[n] * share + q) for n in hops]
        for n in hops:
            total = sums[n]
            if four:
                far_copy(1 - n, q).wait_recv()
                rows = width // 2
                passing_by = part_in[2, q, (1 - n) * rows:(2 - n) * rows, :].astype(F32)
                parts = [total[:rows], total[rows:]]
                parts[1 - n] = parts[1 - n] + passing_by
                total = jnp.concatenate(parts, axis=0)
            part_out[n, q] = total.astype(BF16)
        for n in hops:
            part_copy(n, q).start()

    def send_head():
        if four:
            loop(share, send_far)
        loop(share, own_part)
        loop(share, send_part)

    def send_tail(k, q):
        parts = [project(k, to_aux(i) * share + q) for i in range(groups)]
        tail_in[k - HEAD][0, q] = parts[0]
        for i in range(1, groups):
            tail_out[k - HEAD][i - 1, q] = parts[i]
        for i in range(1, groups):
            tail_copy(k, i, q).start()

    for k in range(CHUNKS):
        loop(clusters - 1, lambda j, k=k: slab_copy(k, far_first(j), from_pair(far_first(j))).wait_recv())
        if k < HEAD - 1:
            loop(pair_count, lambda p, k=k: project_head(k, p))
        elif k == HEAD - 1:
            send_head()
        else:
            loop(share, lambda q, k=k: send_tail(k, q))

    def split_copy(t, i, q, source):
        return remote(
            split[t].at[to_aux(i), q], quarter[t].at[source * share + q],
            split_send.at[t, i, q], split_recv.at[t, i, q], aux=to_aux(i),
        )

    def z_copy(t, i, source):
        return remote(
            zout[t].at[to_pair(i)], zin[t].at[source], z_send.at[t, i], z_recv.at[t, i],
            pair=to_pair(i),
        )

    def f_copy(t, n, j, source):
        member = from_pair(j)
        return remote(
            zin[t].at[member], fetched.at[member, source], f_send.at[t, n, j], f_recv.at[t, n, j],
            aux=near[n],
        )

    def f_pass(t, n, j, source):
        piece_of = half_of(fetched.at[from_pair(j), source], n)
        return remote(
            piece_of, piece_of, f_send.at[t, 2 + n, j], f_recv.at[t, 2 + n, j], aux=near[1 - n]
        )

    def weight(q):
        return live[row * share + q].astype(F32)

    def set_half(t, q, value):
        rounded = value.astype(BF16)
        half[q] = rounded
        for b in range(groups):
            split[t][b, q] = rounded[b * piece:(b + 1) * piece]
        for i in range(1, groups):
            split_copy(t, i, q, row).start()
        quarter[t][row * share + q] = split[t][row, q]

    def start_amplitude(q):
        total = coulomb[q]
        lefts, rights = [], []
        for k in range(HEAD, CHUNKS):
            count = starts[k + 1] - starts[k]
            for i in range(groups):
                if i:
                    tail_copy(k, i, q).wait_recv()
                lefts.append(tail_in[k - HEAD][i, q, :count, :])
                rights.append(tail_in[k - HEAD][i, q, count:, :])
        total = total + dot(jnp.concatenate(lefts, 0), jnp.concatenate(rights, 0), (0, 0))
        coulomb[q] = total
        coulomb_half[q] = total.astype(BF16)
        value = -weight(q) * total * rden[q]
        amp[q] = value
        set_half(0, q, value)

    def add_parts(q):
        total = coulomb[q]
        for n in hops:
            part_copy(n, q).wait_recv()
            total = total + part_in[n, q].astype(F32)
        coulomb[q] = total

    loop(share, add_parts)
    loop(share, start_amplitude)

    def out_copy(n, q, source):
        return remote(
            half.at[q], out_hbm.at[source * share + q], out_send.at[n, q], out_recv.at[n, q],
            aux=near[n],
        )

    def pass_copy(n, q, source):
        piece_of = half_of(out_hbm.at[source * share + q], n)
        return remote(
            piece_of, piece_of, pass_send.at[n, q], pass_recv.at[n, q], aux=near[1 - n]
        )

    for t in range(ITERS):
        def quadratic(q):
            product = dot(half[q], coulomb_half[q], (1, 1)).astype(BF16)
            settled = dot(product, half[q], (1, 0)) * (1.0 / width)
            before = amp[q]
            residual = coulomb[q] + denom[q] * before + settled
            amp[q] = before - damping * residual * rden[q]

        for i in range(1, groups):
            loop(share, lambda q, t=t, i=i: split_copy(t, i, q, from_aux(i)).wait_recv())

        def send_z(j, t=t):
            i = far_first(j)
            to = to_pair(i)
            zout[t][to] = quarter[t][table[clusters + to]]
            z_copy(t, i, cluster).start()

        loop(clusters - 1, send_z)
        mine = quarter[t][table[clusters + cluster]]
        zin[t][cluster] = mine
        fetched[cluster, row] = mine
        for n in hops:
            f_copy(t, n, 0, row).start()
        loop(share, quadratic)

        def hand_on(j, t=t):
            for n in hops:
                f_copy(t, n, j, senders[n]).wait_recv()
                if four:
                    f_pass(t, n, j, near[n]).start()

        def forward(j, t=t):
            j = j + 1
            member = from_pair(j)
            z_copy(t, j, member).wait_recv()
            for n in hops:
                f_copy(t, n, j, row).start()
            fetched[member, row] = zin[t][member]
            hand_on(j - 1)

        loop(clusters - 1, forward)
        hand_on(clusters - 1)
        if t == 0:
            inter_own.wait()
            for i in range(1, groups):
                loop(share, lambda q, i=i: inter_copy(i, q, from_aux(i)).wait_recv())
        if four:
            for n in hops:
                loop(clusters, lambda j, t=t, n=n: f_pass(t, n, j, far).wait_recv())
                loop(clusters, lambda j, t=t, n=n: f_pass(t, n, j, near[n]).wait_send())

        def update(q, t=t):
            p = cluster * pair_count + row * share + q
            rotated = []
            for r in range(ref_cols):
                partner = fetched[refs[r, p] // pair_count].reshape(width, width)
                overlap = inter[r // local_cols, q, r % local_cols]
                rotated.append(dot(overlap, partner, (1, 0)).astype(BF16))
            coupled = jnp.zeros((width, width), F32)
            for r in range(ref_cols):
                overlap = inter[r // local_cols, q, r % local_cols]
                coupled = coupled + dot(rotated[r], overlap, (1, 1))
            value = amp[q] + damping * coupled * rden[q]
            value = weight(q) * value
            if t < ITERS - 1:
                amp[q] = value
                set_half(t + 1, q, value)
            else:
                half[q] = value.astype(BF16)
                for n in hops:
                    out_copy(n, q, row).start()
                total = jnp.sum(coulomb[q] * value, axis=0, keepdims=True)
                energy_row[q] = total

        loop(share, update)

    out_own = pltpu.make_async_copy(half, out_hbm.at[pl.ds(row * share, share)], maps_sem.at[2])
    out_own.start()

    def e_copy(i, source):
        return remote(
            energy_row, energy_out.at[pl.ds(source * share, share)], e_send.at[i], e_recv.at[i], aux=to_aux(i)
        )

    for i in range(1, groups):
        e_copy(i, row).start()
    energy_out[pl.ds(row * share, share)] = energy_row[...]

    def passing(q):
        for n in hops:
            out_copy(n, q, senders[n]).wait_recv()
            if four:
                pass_copy(n, q, near[n]).start()

    loop(share, passing)

    for k in range(CHUNKS):
        loop(clusters - 1, lambda j, k=k: slab_copy(k, j + 1, cluster).wait_send())
    for i in range(1, groups):
        loop(share, lambda q, i=i: inter_copy(i, q, row).wait_send())
        for k in range(HEAD, CHUNKS):
            loop(share, lambda q, i=i, k=k: tail_copy(k, i, q).wait_send())
    for t in range(ITERS):
        loop(clusters - 1, lambda j, t=t: z_copy(t, j + 1, cluster).wait_send())
        for i in range(1, groups):
            loop(share, lambda q, t=t, i=i: split_copy(t, i, q, row).wait_send())
        for n in hops:
            loop(clusters, lambda j, t=t, n=n: f_copy(t, n, j, row).wait_send())
    for i in range(1, groups):
        e_copy(i, row).wait_send()
        e_copy(i, from_aux(i)).wait_recv()
    out_own.wait()
    for n in hops:
        loop(share, lambda q, n=n: part_copy(n, q).wait_send())
        if four:
            loop(share, lambda q, n=n: far_copy(n, q).wait_send())
        loop(share, lambda q, n=n: out_copy(n, q, row).wait_send())
        if four:
            loop(share, lambda q, n=n: pass_copy(n, q, near[n]).wait_send())
            loop(share, lambda q, n=n: pass_copy(n, q, 3 - row).wait_recv())


def on_device(
    orbital_slabs, pno_maps, intersections, pno_energy, occ_energy, pair_orbitals, partners, live
):
    clusters = lax.axis_size("pair")
    groups = lax.axis_size("aux")
    _, aux_rows, virt = orbital_slabs.shape
    pair_count, _, width = pno_maps.shape
    cols = intersections.shape[1]
    share = pair_count // groups
    unit = aux_rows // sum(PARTS)
    head_rows = sum(PARTS[:HEAD]) * unit
    tails = [2 * part * unit for part in PARTS[HEAD:]]
    piece = width // groups
    square = (width, width)
    vm = pltpu.VMEM
    dma = lambda *shape: pltpu.SemaphoreType.DMA(shape)
    scratch = (
        [vm((clusters, part * unit, virt), BF16) for part in PARTS] * 2
        + [vm((groups - 1, share, rows, width), BF16) for rows in tails]
        + [vm((groups, share, rows, width), BF16) for rows in tails]
        + [
            pltpu.SMEM((2 * clusters,), jnp.int32),
            vm((pair_count, virt, width), BF16),
            vm((groups, share, cols) + square, BF16),
            vm((pair_count, head_rows, width), BF16),
            vm((pair_count, head_rows, width), BF16),
            vm((groups - 1, share) + square, BF16),
            vm((groups - 1, share) + square, BF16),
            vm((share,) + square, F32),
            vm((share,) + square, BF16),
            vm((share,) + square, F32),
            vm((share,) + square, F32),
            vm((share,) + square, F32),
            vm((share,) + square, BF16),
            vm((share, 1, width), F32),
        ]
        + [vm((groups, share, piece, width), BF16)] * ITERS
        + [vm((pair_count, piece, width), BF16)] * ITERS
        + [vm((clusters, piece, width), BF16)] * (2 * ITERS)
        + [vm((clusters, groups, piece, width), BF16)]
        + [
            dma(3), dma(groups, share), dma(groups, share), dma(CHUNKS, clusters), dma(CHUNKS, clusters),
            dma(groups, share), dma(groups, share), dma(CHUNKS - HEAD, groups, share),
            dma(CHUNKS - HEAD, groups, share), dma(ITERS, groups, share), dma(ITERS, groups, share),
            dma(ITERS, clusters), dma(ITERS, clusters), dma(ITERS, groups, clusters),
            dma(ITERS, groups, clusters), dma(groups, share), dma(groups, share), dma(groups, share),
            dma(groups, share), dma(groups),
            dma(groups),
        ]
    )
    smem = pl.BlockSpec(memory_space=pltpu.SMEM)
    vmem = pl.BlockSpec(memory_space=pltpu.VMEM)
    anywhere = pl.BlockSpec(memory_space=pl.ANY)
    result, energy = pl.pallas_call(
        functools.partial(kernel, groups, clusters),
        out_shape=(
            jax.ShapeDtypeStruct((pair_count,) + square, BF16),
            jax.ShapeDtypeStruct((pair_count, 1, width), F32),
        ),
        in_specs=[smem] * 4 + [vmem, vmem, anywhere, anywhere],
        out_specs=(anywhere, vmem),
        scratch_shapes=scratch,
        compiler_params=pltpu.CompilerParams(
            collective_id=0, has_side_effects=True, vmem_limit_bytes=62 << 20
        ),
        name="local_pair_amplitudes",
    )(
        pair_orbitals.T, partners.T, live, occ_energy, orbital_slabs, pno_energy, pno_maps,
        intersections,
    )
    return result, jnp.sum(energy, axis=(1, 2))


def solution(mesh):
    placed = (
        P("pair", "aux", None),
        P("pair", None, None),
        P("pair", "aux", None, None),
        P("pair", None),
        P(),
        P(),
        P(),
        P("pair"),
    )
    return jax.shard_map(
        on_device,
        mesh=mesh,
        in_specs=placed,
        out_specs=(P("pair", None, None), P("pair")),
        check_vma=False,
    )
```
